512 devices in a mesh: exp: 64 (over x, y, core), et: 8 (over z).
Axes of the slice: x: 4, y: 8, z: 8, core: 2. Of those that a mesh axis runs over, the one named last changes fastest.
Arguments:
- out_grad: bfloat16 [4096, 2048], P('exp', 'et'), may hold values from -1.5 to 1.5
- gate_scores: float32 [4096, 8], P('exp'), may hold values from 0.1 to 1
- expert_ids: int32 [4096, 8], P('exp'), may hold values from 0 to 63, all different within a row; in each aligned block of 64 rows (0 to 63, 64 to 127, ...) at most 16 rows name the same one
- routed_rows: bfloat16 [64, 1024, 2048], P('exp', None, 'et'), may hold values from -6 to 6
- gate_pre: bfloat16 [64, 768, 1024], P('exp', 'et'), may hold values from -6 to 6
- up_pre: bfloat16 [64, 768, 1024], P('exp', 'et'), may hold values from -6 to 6
- gate_weight: bfloat16 [64, 768, 2048], P('exp', 'et'), may hold values from -0.125 to 0.125
- up_weight: bfloat16 [64, 768, 2048], P('exp', 'et'), may hold values from -0.125 to 0.125
- down_weight: bfloat16 [64, 768, 2048], P('exp', 'et'), may hold values from -0.21875 to 0.21875
Outputs:
- token_grad: bfloat16 [4096, 2048], P('exp', 'et')
- score_grad: float32 [4096, 8], P('exp')
- gate_weight_grad: bfloat16 [64, 768, 2048], P('exp', 'et')
- up_weight_grad: bfloat16 [64, 768, 2048], P('exp', 'et')
- down_weight_grad: bfloat16 [64, 768, 2048], P('exp', 'et')
The draws below stay inside these ranges and needn't reach their ends.
Inputs may be any that keep to these rules, and one draw needn't show every extreme that they name: `expert_ids`: within each block of 64 tokens (the tokens of one index of exp) no expert is named more than 16 times, and in every draw some block names some expert exactly 16 times; each token names 8 different experts.
All inputs are finite; a program needn't handle non-finite values.
Results may differ from the reference program's by a relative error of at most 0.018.
Values may be sent and summed in bfloat16 or wider, within the bound.
A program may use at most 64 MiB of HBM per device.

```python
import math
import jax
import jax.numpy as jnp
import numpy as np
from jax import lax

D = 2048
FF = 768
TOPK = 8
TOK_DEV = 64
EXPERTS = 64
MOST = 16
SLOTS = 1024
TOKENS = 4096
N_EXP = 64


def steps_of(stream_key, extent, shards, least, high):
    gain = 1.0
    for position, parts in shards:
        heights = jax.random.uniform(jax.random.fold_in(jax.random.fold_in(stream_key, 6), position), (parts,), jnp.float32, least / len(shards), high / len(shards))
        gain = gain * jnp.repeat(jnp.exp(heights), extent[position] // parts).reshape((-1,) + (1,) * (len(extent) - 1 - position))
    return gain


def shared_out(key, own, number, rows, count, top, reach, skew):
    ranking = jax.random.permutation(key, count)
    packed, ordinary = load_shares(count, rows * top, reach, skew, True), load_shares(count, rows * top, reach, skew, False)
    places = jnp.arange(count)

    def named(tallies, offset_by):
        used = int((tallies > 0).sum())
        fixed = max(1, used // 4)
        passed = fixed + (places - fixed + offset_by * (used - fixed)) % max(1, count - fixed)
        return jnp.zeros((count,), jnp.int32).at[ranking[jnp.where(places < fixed, places, passed)]].set(jnp.asarray(tallies, jnp.int32))

    tallies = jnp.where(number % 4 == 0, named(packed, number // 4), named(ordinary, number - number // 4 - 1))
    mixed = jax.random.permutation(jax.random.fold_in(own, 3), count)
    giver, sink = mixed[0:count // 2 * 2:2], mixed[1:count // 2 * 2:2]
    room = jnp.minimum(tallies[giver] - 1, reach - tallies[sink]) // 2
    room = jnp.where((giver == ranking[0]) | (sink == ranking[0]) | (tallies[sink] == 0), 0, jnp.maximum(room, 0))
    passed = jax.random.randint(jax.random.fold_in(own, 4), (count // 2,), 0, 1 << 20) % (room + 1)
    tallies = tallies.at[giver].add(-passed).at[sink].add(passed)
    members = jnp.searchsorted(jnp.cumsum(tallies), jnp.arange(rows * top), side="right").astype(jnp.int32)
    grid = members.reshape(top, rows).T
    grid = grid[jax.random.permutation(jax.random.fold_in(own, 1), rows)]
    offset_by = jax.random.randint(jax.random.fold_in(own, 2), (rows, 1), 0, top)
    return jnp.take_along_axis(grid, (jnp.arange(top)[None, :] + offset_by) % top, axis=1)


def load_shares(amount, total, most, lean, full):
    portions = [(1 << 20) // math.isqrt(rank ** lean) + 1 for rank in range(1, amount + 1)]
    largest = most if full else min(most, max(-(-total // amount), total * portions[0] // sum(portions)))
    least = 1 if total - largest >= amount - 1 else 0
    holding, surplus = [largest] + [least] * (amount - 1), total - largest - least * (amount - 1)
    while surplus > 0:
        candidates = [i for i in range(1, amount) if holding[i] < largest] or [i for i in range(1, amount) if holding[i] < most]
        mass, remaining = sum([portions[i] for i in candidates]), surplus
        for i in candidates:
            addition = min(most - holding[i], max(1, remaining * portions[i] // mass), surplus)
            holding[i] = holding[i] + addition
            surplus = surplus - addition
    return np.array(holding)


def scatter_about(stream_key, dims, scale, most, split=(), held_as=jnp.bfloat16):
    level = steps_of(stream_key, dims, split, -0.22, 0.18) if split else 1.0
    values = jax.random.normal(stream_key, dims, jnp.float32) * scale * level
    return jnp.minimum(jnp.maximum(values, -most), most).astype(held_as)


def setup_inputs(seed: int = 0) -> dict:
    key_of = jax.random.split(jax.random.key(seed), 10)
    out_grad = scatter_about(key_of[0], (TOKENS, D), 0.25, 1.5, ((0, 64), (1, 8)))
    gate_scores = jnp.clip(0.1 + 0.9 * jax.random.uniform(key_of[1], (TOKENS, TOPK), jnp.float32) ** steps_of(key_of[1], (TOKENS, TOPK), ((0, 64),), -0.2, 0.2), 0.1, 1.0)
    expert_ids_keys = jax.random.split(jax.random.fold_in(key_of[2], 1), TOKENS // TOK_DEV)
    expert_ids_turns = jax.random.permutation(jax.random.fold_in(key_of[2], 3), TOKENS // TOK_DEV)
    expert_ids = jax.vmap(lambda own, number: shared_out(jax.random.fold_in(key_of[2], 2), own, number, TOK_DEV, EXPERTS, TOPK, MOST, 2))(expert_ids_keys, expert_ids_turns).reshape((TOKENS, TOPK))
    routed_rows = scatter_about(key_of[3], (EXPERTS, SLOTS, D), 1.0, 6.0, ((0, 64), (2, 8)))
    gate_pre = scatter_about(key_of[4], (EXPERTS, FF, SLOTS), 1.0, 6.0, ((0, 64), (1, 8)))
    up_pre = scatter_about(key_of[5], (EXPERTS, FF, SLOTS), 1.0, 6.0, ((0, 64), (1, 8)))
    gate_weight = scatter_about(key_of[6], (EXPERTS, FF, D), D ** -0.5, 0.125, ((0, 64), (1, 8)))
    up_weight = scatter_about(key_of[7], (EXPERTS, FF, D), D ** -0.5, 0.125, ((0, 64), (1, 8)))
    down_weight = scatter_about(key_of[8], (EXPERTS, FF, D), FF ** -0.5, 0.21875, ((0, 64), (1, 8)))
    return {"out_grad": out_grad, "gate_scores": gate_scores, "expert_ids": expert_ids, "routed_rows": routed_rows, "gate_pre": gate_pre, "up_pre": up_pre, "gate_weight": gate_weight, "up_weight": up_weight, "down_weight": down_weight}


def slot_index(expert_ids):
    blocks = expert_ids.reshape(N_EXP, TOK_DEV * TOPK)
    labels = jnp.arange(EXPERTS, dtype=jnp.int32)
    onehot = (blocks[:, :, None] == labels[None, None, :]).astype(jnp.int32)
    earlier = jnp.cumsum(onehot, axis=1) - onehot
    slot_rank = jnp.sum(earlier * onehot, axis=2)
    source = jnp.arange(N_EXP, dtype=jnp.int32)[:, None]
    return (blocks * SLOTS + source * MOST + slot_rank).reshape(-1).astype(jnp.int32)


def expert_backward(items):
    saved_rows, gate_in, up_in, w_gate, w_up, w_down, row_grad, row_score = items
    hidden_raw = jnp.dot(w_down, row_grad.T, preferred_element_type=jnp.float32)
    gate_val = gate_in.astype(jnp.float32)
    up_val = up_in.astype(jnp.float32)
    sigma = jax.nn.sigmoid(gate_val)
    silu_val = gate_val * sigma
    hidden = (silu_val * up_val).astype(jnp.bfloat16)
    score_part = jnp.sum(hidden.astype(jnp.float32) * hidden_raw, axis=0)
    hidden_grad = row_score[None, :] * hidden_raw
    gate_grad = (hidden_grad * up_val * sigma * (1.0 + gate_val * (1.0 - sigma))).astype(jnp.bfloat16)
    up_grad = (hidden_grad * silu_val).astype(jnp.bfloat16)
    scaled_grad = (row_score[:, None] * row_grad.astype(jnp.float32)).astype(jnp.bfloat16)
    down_out = jnp.dot(hidden, scaled_grad, preferred_element_type=jnp.float32).astype(jnp.bfloat16)
    gate_out = jnp.dot(gate_grad, saved_rows, preferred_element_type=jnp.float32).astype(jnp.bfloat16)
    up_out = jnp.dot(up_grad, saved_rows, preferred_element_type=jnp.float32).astype(jnp.bfloat16)
    input_rows = jnp.dot(gate_grad.T, w_gate, preferred_element_type=jnp.float32)
    input_rows = input_rows + jnp.dot(up_grad.T, w_up, preferred_element_type=jnp.float32)
    return gate_out, up_out, down_out, input_rows.astype(jnp.bfloat16), score_part


def reference(out_grad, gate_scores, expert_ids, routed_rows, gate_pre, up_pre, gate_weight, up_weight, down_weight):
    flat_slot = slot_index(expert_ids)
    repeated = jnp.repeat(out_grad, TOPK, axis=0)
    row_grad = jnp.zeros((EXPERTS * SLOTS, D), out_grad.dtype).at[flat_slot].set(repeated)
    row_grad = row_grad.reshape(EXPERTS, SLOTS, D)
    row_score = jnp.zeros((EXPERTS * SLOTS,), jnp.float32).at[flat_slot].set(gate_scores.reshape(-1))
    row_score = row_score.reshape(EXPERTS, SLOTS)
    gate_out, up_out, down_out, input_rows, score_part = lax.map(
        expert_backward,
        (routed_rows, gate_pre, up_pre, gate_weight, up_weight, down_weight, row_grad, row_score))
    picked = input_rows.reshape(EXPERTS * SLOTS, D)[flat_slot].reshape(TOKENS, TOPK, D)
    token_grad = jnp.sum(picked.astype(jnp.float32), axis=1).astype(jnp.bfloat16)
    score_grad = score_part.reshape(-1)[flat_slot].reshape(TOKENS, TOPK)
    return token_grad, score_grad, gate_out, up_out, down_out
```

```python
import functools

import jax
import jax.numpy as jnp
from jax import lax
from jax.experimental import pallas as pl
from jax.experimental.pallas import tpu as pltpu
from jax.sharding import PartitionSpec as P

MESH = pl.DeviceIdType.MESH
BF = jnp.bfloat16
F32 = jnp.float32
NX, NY, NC, NZ, NE = 4, 8, 2, 8, 64
TOK, TOP, W, D, FZ, FF = 64, 8, 256, 2048, 96, 768
META = 512
NR = 528
RA = (0, 320)
RAH = ((0, 160), (160, 160))
RB = (320, 208)
RBH = ((320, 96), (416, 112))
DIRS = (0, 1)


def dot(a, b, dims=((1,), (0,)), precision=None):
    return lax.dot_general(
        a, b, (dims, ((), ())), preferred_element_type=F32, precision=precision
    )


def remote(src, dst, send, recv, target):
    return pltpu.make_async_remote_copy(
        src_ref=src, dst_ref=dst, send_sem=send, recv_sem=recv,
        device_id=target, device_id_type=MESH,
    )


def kernel(
    x_ref, meta_ref, ids_ref, rr_ref, gp_ref, up_ref, gw_ref, uw_ref, dw_ref,
    tg_ref, sg_ref, gg_ref, ug_ref, dg_ref,
    tok, wc, rrp, gup, row_grad, hsp, gfull, sp, stot, acc, wsend, wrecv, rsend, back, sback,
    lsem, zs, zr, ws, wr, ays, ayr, axs, axr, bxs, bxr, bys, byr, prs, prr,
    czs, czr, sps, spr, gs, gr, rs, rr_sem, ss, sr,
):
    e = lax.axis_index("exp")
    z = lax.axis_index("et")
    x = e // 16
    y = lax.rem(e // 2, NY)
    c = lax.rem(e, 2)

    def zz(d):
        return lax.rem(z + d + 16, NZ)

    def yy(d):
        return lax.rem(y + d + 16, NY)

    def xx(d):
        return lax.rem(x + d + 8, NX)

    def at_xy(dx, dy, core):
        return {"exp": (xx(dx) * NY + yy(dy)) * 2 + core}

    barrier = pltpu.get_barrier_semaphore()
    for d in range(1, NZ):
        pl.semaphore_signal(barrier, inc=1, device_id={"et": zz(d)}, device_id_type=MESH)

    def greet(d, carry):
        pl.semaphore_signal(
            barrier, inc=1, device_id={"exp": lax.rem(e + d, NE)}, device_id_type=MESH
        )
        return carry

    lax.fori_loop(1, NE, greet, 0)

    local = [
        pltpu.make_async_copy(x_ref, tok.at[y, x, c, pl.ds(z * TOK, TOK)], lsem.at[0]),
        pltpu.make_async_copy(meta_ref, tok.at[y, x, c, pl.ds(META, 16)], lsem.at[1]),
        pltpu.make_async_copy(gw_ref.at[:, pl.ds(z * W, W)], wc.at[0, z], lsem.at[2]),
        pltpu.make_async_copy(uw_ref.at[:, pl.ds(z * W, W)], wc.at[1, z], lsem.at[3]),
    ]
    for b in range(NY):
        local.append(pltpu.make_async_copy(rr_ref.at[:, b], rrp.at[b], lsem.at[4 + b]))
    for k in local:
        k.start()
    pl.semaphore_wait(barrier, NZ - 1 + NE - 1)

    pend = []

    def go(k):
        k.start()
        pend.append(k)

    ztok = []
    for d in (1, 7, 2, 6, 3, 5, 4):
        k = remote(
            x_ref, tok.at[y, x, c, pl.ds(z * TOK, TOK)], zs.at[d], zr.at[d], {"et": zz(d)}
        )
        go(k)
        ztok.append(k)
    wcols = []
    for d in (1, 7, 2, 6, 3, 5, 4):
        t = zz(d)
        for i, ref in enumerate((gw_ref, uw_ref)):
            k = remote(
                ref.at[:, pl.ds(t * W, W)], wc.at[i, z], ws.at[i, d], wr.at[i, d], {"et": t}
            )
            go(k)
            wcols.append(k)
    for k in local:
        k.wait()

    def permute(b, carry):
        q = lax.broadcasted_iota(jnp.int32, (1024, 128), 0)
        p = lax.broadcasted_iota(jnp.int32, (1024, 128), 1)
        sel = (q == (p // 32) * 256 + b * 32 + lax.rem(p, 32)).astype(F32).astype(BF)
        gup[b, 0:FZ] = dot(gp_ref[...], sel).astype(BF)
        gup[b, FZ : 2 * FZ] = dot(up_ref[...], sel).astype(BF)
        return carry

    lax.fori_loop(0, NY, permute, 0)
    for k in ztok:
        k.wait_recv()

    def sgn(direction):
        return -1 if direction == 0 else 1

    def to_y(direction):
        return at_xy(0, -sgn(direction), c)

    def to_x(direction):
        return at_xy(-sgn(direction), 0, c)

    def a_y(d, s):
        r = RAH[d] if s == 4 else RA
        sl = tok.at[yy(sgn(d) * (s - 1)), x, c, pl.ds(*r)]
        return remote(sl, sl, ays.at[d, s], ayr.at[d, s], to_y(d))

    def a_x(d, g, s):
        r = RAH[d] if s == 2 else RA
        sl = tok.at[yy(g), xx(sgn(d) * (s - 1)), c, pl.ds(*r)]
        return remote(sl, sl, axs.at[d, g % 8, s], axr.at[d, g % 8, s], to_x(d))

    def b_x(d, s):
        r = RBH[d] if s == 2 else RB
        sl = tok.at[y, xx(sgn(d) * (s - 1)), c, pl.ds(*r)]
        return remote(sl, sl, bxs.at[d, s], bxr.at[d, s], to_x(d))

    def b_y(d, q, s):
        r = RBH[d] if s == 4 else RB
        sl = tok.at[yy(sgn(d) * (s - 1)), xx(q), c, pl.ds(*r)]
        return remote(sl, sl, bys.at[d, q % 4, s], byr.at[d, q % 4, s], to_y(d))

    def pair(g):
        sl = tok.at[yy(g), :, c]
        return remote(sl, sl, prs.at[g % 8], prr.at[g % 8], at_xy(0, 0, 1 - c))

    def c_z(d, g, s):
        sl = gfull.at[yy(g), zz(sgn(d) * (s - 1))]
        if s == 4:
            sl = sl.at[pl.ds(d * FZ, FZ)]
        return remote(
            sl, sl, czs.at[d, g % 8, s], czr.at[d, g % 8, s], {"et": zz(-sgn(d))}
        )

    def compute(g):
        pair(g).wait_recv()
        b = yy(g)
        lane = lax.broadcasted_iota(jnp.int32, (1, W), 1)
        ui = lax.broadcasted_iota(jnp.int32, (W, W), 0)
        uj = lax.broadcasted_iota(jnp.int32, (W, W), 1)
        upper = ((ui < uj) & (ui // TOK == uj // TOK)).astype(F32).astype(BF)
        srow = jnp.zeros((8, 128), F32)
        picks = []
        for h in range(2):
            mt = tok[b, 2 * h : 2 * h + 2, :, META : META + 16, :].reshape(4, 16, W).astype(F32)
            hit = (mt[:, 0:8, :] == (e + 1).astype(F32)).astype(F32)
            m = jnp.sum(hit, axis=(0, 1))[None]
            sv = jnp.sum(hit * mt[:, 8:16, :], axis=(0, 1))[None]
            rank = dot(jnp.broadcast_to(m, (8, W)).astype(BF), upper)[0:1]
            want = jnp.where(m > 0, rank.astype(jnp.int32) + 16 * (lane // TOK) + 64 * h, -1)
            slot = lax.broadcasted_iota(jnp.int32, (128, W), 0)
            pick = (slot == want).astype(F32).astype(BF)
            picks.append(pick)
            srow += dot(jnp.broadcast_to(sv, (8, W)).astype(BF), pick, ((1,), (1,)))
        srow = srow[0:1]
        hr = jnp.zeros((FZ, 128), F32)
        for f in range(NZ):
            rows = jnp.zeros((128, W), F32)
            for h in range(2):
                part = tok[b, 2 * h : 2 * h + 2, :, f * TOK : (f + 1) * TOK, :].reshape(W, W)
                rows += dot(picks[h], part)
            rows = rows.astype(BF)
            row_grad[b, :, f * W : (f + 1) * W] = rows
            hr += dot(dw_ref[:, f * W : (f + 1) * W], rows, ((1,), (1,)))
        gate = gup[b, 0:FZ].astype(F32)
        up = gup[b, FZ : 2 * FZ].astype(F32)
        sig = jax.nn.sigmoid(gate)
        silu = gate * sig
        hidden = (silu * up).astype(BF).astype(F32)
        sp[z, pl.ds(b, 1), :] = jnp.sum(hidden * hr, axis=0, keepdims=True)
        hg = srow * hr
        gfull[b, z, 0:FZ] = (hg * up * sig * (1.0 + gate * (1.0 - sig))).astype(BF)
        gfull[b, z, FZ : 2 * FZ] = (hg * silu).astype(BF)
        hsp[b] = (hidden * srow).astype(BF)
        for d in DIRS:
            go(c_z(d, g, 1))

    def advance(g, s):
        for d in DIRS:
            c_z(d, g, s).wait_recv()
            if s < 4:
                go(c_z(d, g, s + 1))

    def weights_part(g, first):
        b = yy(g)
        for i in range(2):
            part = dot(gfull[b, :, i * FZ : (i + 1) * FZ, :].reshape(FF, 128), rrp[b].reshape(128, W))
            if first:
                acc[i] = part
            else:
                acc[i] += part

    def rows_part(g):
        b = yy(g)
        out = dot(gfull[b, :, 0:FZ, :].reshape(FF, 128), wc[0].reshape(FF, W), ((0,), (0,)))
        out += dot(
            gfull[b, :, FZ : 2 * FZ, :].reshape(FF, 128), wc[1].reshape(FF, W), ((0,), (0,))
        )
        rsend[b] = out.astype(BF).reshape(NX, NC, 16, W)

    for d in DIRS:
        go(b_x(d, 1))
    for d in DIRS:
        go(a_y(d, 1))
    for d in DIRS:
        go(a_x(d, 0, 1))
    for d in DIRS:
        go(b_y(d, 0, 1))
    for d in DIRS:
        b_x(d, 1).wait_recv()
        go(b_x(d, 2))
    for q in (-1, 1):
        for d in DIRS:
            go(b_y(d, q, 1))
    for d in DIRS:
        b_x(d, 2).wait_recv()
    for d in DIRS:
        go(b_y(d, 2, 1))

    def groups(k):
        return [0] if k == 0 else ([4] if k == 4 else [k, -k])

    order = []
    for k in range(5):
        order += groups(k)

    def step_bx(q, k):
        for d in DIRS:
            b_y(d, q, k).wait_recv()
            if k < 4:
                go(b_y(d, q, k + 1))

    def step_ax(g):
        for d in DIRS:
            a_x(d, g, 1).wait_recv()
            go(a_x(d, g, 2))

    def finish(g):
        for d in DIRS:
            a_x(d, g, 2).wait_recv()
        go(pair(g))

    for k in range(1, 5):
        for d in DIRS:
            a_y(d, k).wait_recv()
            if k < 4:
                go(a_y(d, k + 1))
                for dd in DIRS:
                    go(a_x(dd, sgn(d) * k, 1))
        if k == 4:
            for dd in DIRS:
                go(a_x(dd, 4, 1))
        prev = groups(k - 1)
        step_bx(0, k)
        step_ax(prev[0])
        step_bx(1, k)
        if len(prev) > 1:
            step_ax(prev[1])
        step_bx(-1, k)
        step_bx(2, k)
        for g in prev:
            finish(g)
    step_ax(4)
    finish(4)

    for g in order:
        compute(g)
    for d in range(1, NZ):
        go(remote(sp.at[z], sp.at[z], sps.at[d], spr.at[d], {"et": zz(d)}))
    for s in range(1, 5):
        for g in order:
            advance(g, s)
    for d in range(1, NZ):
        remote(sp.at[z], sp.at[z], sps.at[d], spr.at[d], {"et": zz(d)}).wait_recv()
    for i, g in enumerate(order):
        weights_part(g, i == 0)

    for i in range(2):
        wsend[i] = acc[i].astype(BF).reshape(NZ, FZ, W)
    wout = []
    for d in (4, 3, 5, 2, 6, 1, 7):
        t = zz(d)
        for i in range(2):
            k = remote(wsend.at[i, t], wrecv.at[i, z], gs.at[i, d], gr.at[i, d], {"et": t})
            go(k)
            wout.append(k)

    total = sp[0]
    for i in range(1, NZ):
        total = total + sp[i]
    stot[...] = total.reshape(NY, 1, 128)
    for k in wcols:
        k.wait_recv()
    for g in order:
        rows_part(g)

    def score_to(d):
        t = lax.rem(e + d, NE)
        ty = lax.rem(t // 2, NY)
        return remote(stot.at[ty], sback.at[e], ss.at[d], sr.at[d], {"exp": t})

    def rows_to(d):
        t = lax.rem(e + d, NE)
        src = rsend.at[lax.rem(t // 2, NY), t // 16, lax.rem(t, 2)]
        return remote(src, back.at[e], rs.at[d], rr_sem.at[d], {"exp": t})

    def send_back(d, carry):
        rows_to(d).start()
        score_to(d).start()
        return carry

    lax.fori_loop(1, NE, send_back, 0)
    keep = [
        pltpu.make_async_copy(rsend.at[y, x, c], back.at[e], lsem.at[0]),
        pltpu.make_async_copy(stot.at[y], sback.at[e], lsem.at[1]),
    ]
    for k in keep:
        k.start()

    hs = jnp.concatenate([hsp[b] for b in range(NY)], axis=1)
    for f in range(NZ):
        rows = row_grad[:, :, f * W : (f + 1) * W].reshape(1024, W)
        dg_ref[:, f * W : (f + 1) * W] = dot(hs, rows).astype(BF)

    ids = ids_ref[...]
    lane_e = lax.broadcasted_iota(jnp.int32, (TOK, NE), 1)
    names = jnp.zeros((TOK, NE), F32)
    for k in range(TOP):
        names += (ids[:, k : k + 1] == lane_e).astype(F32)
    ti = lax.broadcasted_iota(jnp.int32, (TOK, TOK), 0)
    tj = lax.broadcasted_iota(jnp.int32, (TOK, TOK), 1)
    rank = dot((tj < ti).astype(F32).astype(BF), names.astype(BF))
    rank = jnp.where(names > 0, rank, -1.0)
    ei = lax.broadcasted_iota(jnp.int32, (NE, 1024), 0)
    ej = lax.broadcasted_iota(jnp.int32, (NE, 1024), 1)
    spread = (ej // 16 == ei).astype(F32).astype(BF)
    place = lax.rem(lax.broadcasted_iota(jnp.int32, (TOK, 1024), 1), 16).astype(F32)
    gather = (dot(rank.astype(BF), spread) == place).astype(F32).astype(BF)

    for k in keep:
        k.wait()

    def wait_back(d, carry):
        rows_to(d).wait_recv()
        score_to(d).wait_recv()
        return carry

    lax.fori_loop(1, NE, wait_back, 0)
    tg_ref[...] = dot(gather, back[...].reshape(1024, W)).astype(BF)
    li = lax.broadcasted_iota(jnp.int32, (16, 128), 0)
    lj = lax.broadcasted_iota(jnp.int32, (16, 128), 1)
    mine = (lj == x * 32 + c * 16 + li).astype(F32)
    slots = dot(mine, sback[...].reshape(NE, 128), ((1,), (1,)), lax.Precision.HIGHEST)
    value = jnp.zeros((TOK, NE), F32)
    for j in range(16):
        value += jnp.where(rank == j, slots[j : j + 1, :], 0.0)
    lane_k = lax.broadcasted_iota(jnp.int32, (TOK, TOP), 1)
    score = jnp.zeros((TOK, TOP), F32)
    for k in range(TOP):
        one = jnp.sum(jnp.where(ids[:, k : k + 1] == lane_e, value, 0.0), axis=1, keepdims=True)
        score = jnp.where(lane_k == k, one, score)
    sg_ref[...] = score

    for i in range(2):
        wrecv[i, z] = wsend[i, z]
    for k in wout:
        k.wait_recv()
    for i, ref in enumerate((gg_ref, ug_ref)):
        for t in range(NZ):
            ref[:, t * W : (t + 1) * W] = wrecv[i, t]

    for k in pend:
        k.wait_send()

    def wait_sent(d, carry):
        rows_to(d).wait_send()
        score_to(d).wait_send()
        return carry

    lax.fori_loop(1, NE, wait_sent, 0)


def body(
    out_grad, gate_scores, expert_ids, routed_rows, gate_pre, up_pre,
    gate_weight, up_weight, down_weight,
):
    e = lax.axis_index("exp")
    lane = lax.rem(e // 16, 2) * 2 + lax.rem(e, 2)
    pair = jnp.concatenate(
        [(expert_ids + 1).astype(F32).T, gate_scores.T], axis=0
    ).astype(BF)
    meta = jnp.where(
        (jnp.arange(W, dtype=jnp.int32) // TOK == lane)[None, :], jnp.tile(pair, (1, 4)), 0
    ).astype(BF)
    vmem = pl.BlockSpec(memory_space=pltpu.VMEM)
    hbm = pl.BlockSpec(memory_space=pl.ANY)
    dma = pltpu.SemaphoreType.DMA
    outs = pl.pallas_call(
        kernel,
        out_shape=(
            jax.ShapeDtypeStruct((TOK, W), BF),
            jax.ShapeDtypeStruct((TOK, TOP), F32),
            jax.ShapeDtypeStruct((FZ, D), BF),
            jax.ShapeDtypeStruct((FZ, D), BF),
            jax.ShapeDtypeStruct((FZ, D), BF),
        ),
        in_specs=[vmem, vmem, vmem, hbm, vmem, vmem, vmem, vmem, vmem],
        out_specs=(vmem,) * 5,
        scratch_shapes=[
            pltpu.VMEM((NY, NX, NC, NR, W), BF),
            pltpu.VMEM((2, NZ, FZ, W), BF),
            pltpu.VMEM((NY, NX, 32, W), BF),
            pltpu.VMEM((NY, 2 * FZ, 128), BF),
            pltpu.VMEM((NY, 128, D), BF),
            pltpu.VMEM((NY, FZ, 128), BF),
            pltpu.VMEM((NY, NZ, 2 * FZ, 128), BF),
            pltpu.VMEM((NZ, NY, 128), F32),
            pltpu.VMEM((NY, 1, 128), F32),
            pltpu.VMEM((2, FF, W), F32),
            pltpu.VMEM((2, NZ, FZ, W), BF),
            pltpu.VMEM((2, NZ, FZ, W), BF),
            pltpu.VMEM((NY, NX, NC, 16, W), BF),
            pltpu.VMEM((NE, 16, W), BF),
            pltpu.VMEM((NE, 1, 128), F32),
            dma((12,)),
            dma((8,)), dma((8,)),
            dma((2, 8)), dma((2, 8)),
            dma((2, 5)), dma((2, 5)),
            dma((2, 8, 3)), dma((2, 8, 3)),
            dma((2, 3)), dma((2, 3)),
            dma((2, 4, 5)), dma((2, 4, 5)),
            dma((8,)), dma((8,)),
            dma((2, 8, 5)), dma((2, 8, 5)),
            dma((8,)), dma((8,)),
            dma((2, 8)), dma((2, 8)),
            dma((NE,)), dma((NE,)),
            dma((NE,)), dma((NE,)),
        ],
        compiler_params=pltpu.CompilerParams(
            collective_id=0, has_side_effects=True, vmem_limit_bytes=56 << 20
        ),
        name="expert_backward",
    )(
        out_grad, meta, expert_ids, routed_rows.reshape(NX, NY, 32, W),
        gate_pre.reshape(FZ, 1024), up_pre.reshape(FZ, 1024),
        gate_weight.reshape(FZ, D), up_weight.reshape(FZ, D), down_weight.reshape(FZ, D),
    )
    token_grad, score_grad, gate_out, up_out, down_out = outs
    return token_grad, score_grad, gate_out[None], up_out[None], down_out[None]


def solution(mesh):
    return jax.shard_map(
        body,
        mesh=mesh,
        in_specs=(
            P("exp", "et"), P("exp", None), P("exp", None), P("exp", None, "et"),
            P("exp", "et", None), P("exp", "et", None), P("exp", "et", None),
            P("exp", "et", None), P("exp", "et", None),
        ),
        out_specs=(
            P("exp", "et"), P("exp", None), P("exp", "et", None), P("exp", "et", None),
            P("exp", "et", None),
        ),
        check_vma=False,
    )
```

```python
import functools

import jax
import jax.numpy as jnp
from jax import lax
from jax.experimental import pallas as pl
from jax.experimental.pallas import tpu as pltpu
from jax.sharding import PartitionSpec as P

MESH = pl.DeviceIdType.MESH
BF = jnp.bfloat16
F32 = jnp.float32
NX, NY, NC, NZ, NE = 4, 8, 2, 8, 64
TOK, TOP, W, D, FZ, FF = 64, 8, 256, 2048, 96, 768
META = 512
NR = 528
RA = (0, 320)
RAH = ((0, 160), (160, 160))
RB = (320, 208)
RBH = ((320, 96), (416, 112))
DIRS = (0, 1)
STEPPED = (0, 1, -1, 2, -2, 3, -3, 4)


def dot(a, b, dims=((1,), (0,)), precision=None):
    return lax.dot_general(
        a, b, (dims, ((), ())), preferred_element_type=F32, precision=precision
    )


def remote(src, dst, send, recv, target):
    return pltpu.make_async_remote_copy(
        src_ref=src, dst_ref=dst, send_sem=send, recv_sem=recv,
        device_id=target, device_id_type=MESH,
    )


def kernel(
    x_ref, ids_ref, score_ref, rr_ref, gp_hbm, up_hbm, gw_ref, uw_ref, dw_hbm,
    tg_ref, sg_ref, gg_ref, ug_ref, dg_ref,
    tok, wc, rrp, gp_ref, up_ref, dw_ref, gup, row_grad, hsp, gfull, sp, stot, acc, wsend, rsend, back, sback,
    lsem, zs, zr, ws, wr, fhs, fhr, ays, ayr, axs, axr, bxs, bxr, bys, byr, prs, prr,
    czs, czr, sps, spr, gs, gr, rs, rr_sem, ss, sr,
):
    e = lax.axis_index("exp")
    z = lax.axis_index("et")
    x = e // 16
    y = lax.rem(e // 2, NY)
    c = lax.rem(e, 2)

    def zz(d):
        return lax.rem(z + d + 16, NZ)

    def yy(d):
        return lax.rem(y + d + 16, NY)

    def xx(d):
        return lax.rem(x + d + 8, NX)

    def at_xy(dx, dy, core):
        return {"exp": (xx(dx) * NY + yy(dy)) * 2 + core}

    barrier = pltpu.get_barrier_semaphore()
    for d in range(1, NZ):
        pl.semaphore_signal(barrier, inc=1, device_id={"et": zz(d)}, device_id_type=MESH)

    near = (at_xy(1, 0, c), at_xy(-1, 0, c), at_xy(0, 1, c), at_xy(0, -1, c), at_xy(0, 0, 1 - c))
    for t in near:
        pl.semaphore_signal(barrier, inc=1, device_id=t, device_id_type=MESH)

    local = [
        pltpu.make_async_copy(x_ref, tok.at[y, x, c, pl.ds(z * TOK, TOK)], lsem.at[0]),
        pltpu.make_async_copy(gp_hbm, gp_ref, lsem.at[1]),
        pltpu.make_async_copy(up_hbm, up_ref, lsem.at[2]),
        pltpu.make_async_copy(dw_hbm, dw_ref, lsem.at[3]),
        pltpu.make_async_copy(gw_ref.at[:, pl.ds(z * W, W)], wc.at[0, z], lsem.at[12]),
        pltpu.make_async_copy(uw_ref.at[:, pl.ds(z * W, W)], wc.at[1, z], lsem.at[13]),
    ]
    for b in range(NY):
        local.append(pltpu.make_async_copy(rr_ref.at[:, b], rrp.at[b], lsem.at[4 + b]))
    for k in local:
        k.start()
    place = lax.rem(x, 2) * 2 + c
    pair_rows = jnp.concatenate(
        [(ids_ref[...] + 1).astype(F32), score_ref[...]], axis=0
    )
    pair_rows = jnp.concatenate([pair_rows] * 4, axis=1)
    lane_block = lax.broadcasted_iota(jnp.int32, (16, W), 1) // TOK
    tok[y, x, c, META : META + 16, :] = jnp.where(lane_block == place, pair_rows, 0.0).astype(BF)
    pl.semaphore_wait(barrier, NZ - 1 + len(near))

    pend = []

    def go(k):
        k.start()
        pend.append(k)

    ztok = {}
    for d in (1, 7, 2, 6, 3, 5, 4):
        k = remote(
            x_ref, tok.at[y, x, c, pl.ds(z * TOK, TOK)], zs.at[d], zr.at[d], {"et": zz(d)}
        )
        go(k)
        ztok[d] = k
    wcols = []

    def send_columns(order):
        for d in order:
            t = zz(d)
            for i, ref in enumerate((gw_ref, uw_ref)):
                k = remote(
                    ref.at[:, pl.ds(t * W, W)], wc.at[i, z], ws.at[i, d], wr.at[i, d], {"et": t}
                )
                go(k)
                wcols.append(k)

    def permute(b, carry):
        q = lax.broadcasted_iota(jnp.int32, (1024, 128), 0)
        p = lax.broadcasted_iota(jnp.int32, (1024, 128), 1)
        sel = (q == (p // 32) * 256 + b * 32 + lax.rem(p, 32)).astype(F32).astype(BF)
        gup[b, 0:FZ] = dot(gp_ref[...], sel).astype(BF)
        gup[b, FZ : 2 * FZ] = dot(up_ref[...], sel).astype(BF)
        return carry

    def sgn(direction):
        return -1 if direction == 0 else 1

    def to_y(direction):
        return at_xy(0, -sgn(direction), c)

    def to_x(direction):
        return at_xy(-sgn(direction), 0, c)

    def a_y(d, s):
        r = RAH[d] if s == 4 else RA
        sl = tok.at[yy(sgn(d) * (s - 1)), x, c, pl.ds(*r)]
        if s == 1:
            return remote(sl, sl, fhs.at[0, d, 0], fhr.at[0, d, 0], to_y(d))
        return remote(sl, sl, ays.at[d, s], ayr.at[d, s], to_y(d))

    def a_x(d, g, s):
        r = RAH[d] if s == 2 else RA
        sl = tok.at[yy(g), xx(sgn(d) * (s - 1)), c, pl.ds(*r)]
        if g == 0 and s == 1:
            return remote(sl, sl, fhs.at[1, d, 0], fhr.at[1, d, 0], to_x(d))
        return remote(sl, sl, axs.at[d, g % 8, s], axr.at[d, g % 8, s], to_x(d))

    def b_x(d, s):
        r = RBH[d] if s == 2 else RB
        sl = tok.at[y, xx(sgn(d) * (s - 1)), c, pl.ds(*r)]
        if s == 1:
            return remote(sl, sl, fhs.at[1, d, 1], fhr.at[1, d, 1], to_x(d))
        return remote(sl, sl, bxs.at[d, s], bxr.at[d, s], to_x(d))

    def b_y(d, q, s):
        r = RBH[d] if s == 4 else RB
        sl = tok.at[yy(sgn(d) * (s - 1)), xx(q), c, pl.ds(*r)]
        if q == 0 and s == 1:
            return remote(sl, sl, fhs.at[0, d, 1], fhr.at[0, d, 1], to_y(d))
        return remote(sl, sl, bys.at[d, q % 4, s], byr.at[d, q % 4, s], to_y(d))

    def pair(g, i):
        sl = tok.at[yy(g), :, c, pl.ds(*(RA, RB)[i])]
        return remote(sl, sl, prs.at[i, g % 8], prr.at[i, g % 8], at_xy(0, 0, 1 - c))

    def c_z(d, g, s):
        relayed = s == 2 and g in STEPPED
        held = 1 if relayed else (0 if s < 3 else 2)
        sl = gfull.at[yy(g), zz(sgn(d) * held)]
        if s == 4:
            sl = sl.at[pl.ds(d * FZ, FZ)]
        far = s - held
        return remote(
            sl, sl, czs.at[d, g % 8, s], czr.at[d, g % 8, s], {"et": zz(-sgn(d) * far)}
        )

    def compute(g):
        for i in range(2):
            pair(g, i).wait_recv()
        b = yy(g)
        lane = lax.broadcasted_iota(jnp.int32, (1, W), 1)
        ui = lax.broadcasted_iota(jnp.int32, (W, W), 0)
        uj = lax.broadcasted_iota(jnp.int32, (W, W), 1)
        upper = ((ui < uj) & (ui // TOK == uj // TOK)).astype(F32).astype(BF)
        srow = jnp.zeros((8, 128), F32)
        picks = []
        for h in range(2):
            mt = tok[b, 2 * h : 2 * h + 2, :, META : META + 16, :].reshape(4, 16, W).astype(F32)
            hit = (mt[:, 0:8, :] == (e + 1).astype(F32)).astype(F32)
            m = jnp.sum(hit, axis=(0, 1))[None]
            sv = jnp.sum(hit * mt[:, 8:16, :], axis=(0, 1))[None]
            rank = dot(jnp.broadcast_to(m, (8, W)).astype(BF), upper)[0:1]
            want = jnp.where(m > 0, rank.astype(jnp.int32) + 16 * (lane // TOK) + 64 * h, -1)
            slot = lax.broadcasted_iota(jnp.int32, (128, W), 0)
            pick = (slot == want).astype(F32).astype(BF)
            picks.append(pick)
            srow += dot(jnp.broadcast_to(sv, (8, W)).astype(BF), pick, ((1,), (1,)))
        srow = srow[0:1]
        hr = jnp.zeros((FZ, 128), F32)
        for f in range(NZ):
            rows = jnp.zeros((128, W), F32)
            for h in range(2):
                part = tok[b, 2 * h : 2 * h + 2, :, f * TOK : (f + 1) * TOK, :].reshape(W, W)
                rows += dot(picks[h], part)
            rows = rows.astype(BF)
            row_grad[b, :, f * W : (f + 1) * W] = rows
            hr += dot(dw_ref[:, f * W : (f + 1) * W], rows, ((1,), (1,)))
        gate = gup[b, 0:FZ].astype(F32)
        up = gup[b, FZ : 2 * FZ].astype(F32)
        sig = jax.nn.sigmoid(gate)
        silu = gate * sig
        hidden = (silu * up).astype(BF).astype(F32)
        sp[z, pl.ds(b, 1), :] = jnp.sum(hidden * hr, axis=0, keepdims=True)
        hg = srow * hr
        gfull[b, z, 0:FZ] = (hg * up * sig * (1.0 + gate * (1.0 - sig))).astype(BF)
        gfull[b, z, FZ : 2 * FZ] = (hg * silu).astype(BF)
        hsp[b] = (hidden * srow).astype(BF)
        for s in (1,) if g in STEPPED else (2, 1):
            for d in DIRS:
                go(c_z(d, g, s))

    def step(g):
        for d in DIRS:
            c_z(d, g, 1).wait_recv()
            go(c_z(d, g, 2))

    def relay(g):
        for d in DIRS:
            c_z(d, g, 2).wait_recv()
            for s in (3, 4):
                go(c_z(d, g, s))

    def collect(g):
        for s in (3, 4) if g in STEPPED else (1, 3, 4):
            for d in DIRS:
                c_z(d, g, s).wait_recv()

    def weights_part(g, first):
        b = yy(g)
        for i in range(2):
            part = dot(gfull[b, :, i * FZ : (i + 1) * FZ, :].reshape(FF, 128), rrp[b].reshape(128, W))
            if first:
                acc[i] = part
            else:
                acc[i] += part

    def rows_part(g):
        b = yy(g)
        out = dot(gfull[b, :, 0:FZ, :].reshape(FF, 128), wc[0].reshape(FF, W), ((0,), (0,)))
        out += dot(
            gfull[b, :, FZ : 2 * FZ, :].reshape(FF, 128), wc[1].reshape(FF, W), ((0,), (0,))
        )
        rsend[b] = out.astype(BF).reshape(NX, NC, 16, W)

    def piece(d, axis, src, rows, part):
        dst = tok.at[y, x, c, rows]
        return remote(
            dst if src is None else src, dst, fhs.at[axis, d, part], fhr.at[axis, d, part],
            (to_y, to_x)[axis](d),
        )

    def send_piece(src, rows, part):
        for axis in (1, 0):
            for d in DIRS:
                piece(d, axis, src, rows, part).start()

    send_piece(None, pl.ds(META, 16), 1)
    send_piece(x_ref, pl.ds(z * TOK, TOK), z // 5)
    for d in (1, 7, 2, 6, 3, 5, 4):
        ztok[d].wait_recv()
        f = zz(-d)
        send_piece(None, pl.ds(f * TOK, TOK), f // 5)
    for d in DIRS:
        pend.extend([a_y(d, 1), a_x(d, 0, 1), b_x(d, 1), b_y(d, 0, 1)])
    send_columns((1, 7, 2, 6, 3, 5, 4))
    for k in local:
        k.wait()
    lax.fori_loop(0, NY, permute, 0)

    order = (0, 1, -1, 2, -2, 3, -3, 4)
    done = []
    unsent = []

    def ax0(g):
        for d in DIRS:
            go(a_x(d, g, 1))

    def ax1(g):
        for d in DIRS:
            a_x(d, g, 1).wait_recv()
            go(a_x(d, g, 2))

    def ay(k):
        for d in DIRS:
            a_y(d, k).wait_recv()
            if k < 4:
                go(a_y(d, k + 1))

    def bx1():
        for d in DIRS:
            b_x(d, 1).wait_recv()
            go(b_x(d, 2))
        for q in (-1, 1):
            for d in DIRS:
                go(b_y(d, q, 1))

    def bx2():
        for d in DIRS:
            b_x(d, 2).wait_recv()
        for d in DIRS:
            go(b_y(d, 2, 1))

    def by(q, k):
        for d in DIRS:
            b_y(d, q, k).wait_recv()
            if k < 4:
                go(b_y(d, q, k + 1))

    def pb(g):
        go(pair(g, 1))

    def fin(g):
        for d in DIRS:
            a_x(d, g, 2).wait_recv()
        go(pair(g, 0))

    def take(g):
        collect(g)
        weights_part(g, not done)
        if not done:
            for k in wcols:
                k.wait_recv()
        rows_part(g)
        done.append(g)
        unsent.append(g)

    comp = compute
    plan = [
        (bx1,),
        (ay, 1),
        (ax0, 1),
        (ax0, -1),
        (bx2,),
        (pb, 0),
        (ax1, 0),
        (ay, 2),
        (ax0, 2),
        (ax0, -2),
        (by, 0, 1),
        (by, 1, 1),
        (fin, 0),
        (ax1, 1),
        (ay, 3),
        (by, -1, 1),
        (by, 2, 1),
        (pb, 1),
        (pb, -1),
        (comp, 0),
        (ax1, -1),
        (ax0, 3),
        (ax0, -3),
        (by, 0, 2),
        (fin, 1),
        (ay, 4),
        (by, 1, 2),
        (ax1, 2),
        (comp, 1),
        (step, 0),
        (by, -1, 2),
        (ax0, 4),
        (fin, -1),
        (by, 2, 2),
        (pb, 2),
        (pb, -2),
        (comp, -1),
        (relay, 0),
        (step, 1),
        (ax1, -2),
        (by, 0, 3),
        (fin, 2),
        (by, 1, 3),
        (ax1, 3),
        (comp, 2),
        (relay, 1),
        (step, -1),
        (by, -1, 3),
        (fin, -2),
        (by, 2, 3),
        (pb, 3),
        (pb, -3),
        (comp, -2),
        (take, 0),
        (relay, -1),
        (step, 2),
        (ax1, -3),
        (by, 0, 4),
        (fin, 3),
        (ax1, 4),
        (by, 1, 4),
        (comp, 3),
        (take, 1),
        (relay, 2),
        (step, -2),
        (by, -1, 4),
        (by, 2, 4),
        (pb, 4),
        (fin, -3),
        (comp, -3),
        (take, -1),
        (relay, -2),
        (step, 3),
        (fin, 4),
        (comp, 4),
        (take, 2),
        (relay, 3),
        (step, -3),
    ]
    for event, *given in plan:
        event(*given)

    def target_rows(t):
        src = rsend.at[lax.rem(t // 2, NY), t // 16, lax.rem(t, 2)]
        return src

    def rows_to(t):
        return remote(target_rows(t), back.at[e], rs.at[t], rr_sem.at[e], {"exp": t})

    def rows_from(t):
        return remote(target_rows(e), back.at[t], rs.at[t], rr_sem.at[t], {"exp": t})

    def score_to(t):
        return remote(
            stot.at[lax.rem(t // 2, NY)], sback.at[e], ss.at[t], sr.at[e], {"exp": t}
        )

    def score_from(t):
        return remote(stot.at[y], sback.at[t], ss.at[t], sr.at[t], {"exp": t})

    def send_rows(g):
        for dx in (0, 1, -1, 2):
            for core in range(2):
                if g == 0 and dx == 0:
                    if core == 0:
                        rows_to(at_xy(0, 0, 1 - c)["exp"]).start()
                    continue
                rows_to(at_xy(dx, g, core)["exp"]).start()

    for d in range(1, NZ):
        go(remote(sp.at[z], sp.at[z], sps.at[d], spr.at[d], {"et": zz(d)}))
    step(4)
    if unsent:
        send_rows(unsent.pop(0))
    relay(-3)
    if unsent:
        send_rows(unsent.pop(0))
    relay(4)
    if unsent:
        send_rows(unsent.pop(0))
    take(-2)
    send_rows(unsent.pop(0))
    take(3)
    send_rows(unsent.pop(0))
    take(-3)
    send_rows(unsent.pop(0))
    take(4)
    for i in range(2):
        wsend[i] = acc[i].astype(BF).reshape(NZ, FZ, W)
    wout = []
    for d in (4, 3, 5, 2, 6, 1, 7):
        t = zz(d)
        for i, ref in enumerate((gg_ref, ug_ref)):
            k = remote(
                wsend.at[i, t], ref.at[:, pl.ds(z * W, W)], gs.at[i, d], gr.at[i, d], {"et": t}
            )
            go(k)
            wout.append(k)
    for g in unsent:
        send_rows(g)
    for d in range(1, NZ):
        remote(sp.at[z], sp.at[z], sps.at[d], spr.at[d], {"et": zz(d)}).wait_recv()
    total = sp[0]
    for i in range(1, NZ):
        total = total + sp[i]
    stot[...] = total.reshape(NY, 1, 128)

    def send_scores(d, carry):
        score_to(lax.rem(e + d, NE)).start()
        return carry

    lax.fori_loop(1, NE, send_scores, 0)
    keep = [
        pltpu.make_async_copy(rsend.at[y, x, c], back.at[e], lsem.at[0]),
        pltpu.make_async_copy(stot.at[y], sback.at[e], lsem.at[1]),
        pltpu.make_async_copy(wsend.at[0, z], gg_ref.at[:, pl.ds(z * W, W)], lsem.at[2]),
        pltpu.make_async_copy(wsend.at[1, z], ug_ref.at[:, pl.ds(z * W, W)], lsem.at[3]),
    ]
    for k in keep:
        k.start()

    hs = jnp.concatenate([hsp[b] for b in range(NY)], axis=1)
    for f in range(NZ):
        rows = row_grad[:, :, f * W : (f + 1) * W].reshape(1024, W)
        dg_ref[:, f * W : (f + 1) * W] = dot(hs, rows).astype(BF)

    ids = ids_ref[...]
    row_e = lax.broadcasted_iota(jnp.int32, (NE, TOK), 0)
    names = jnp.zeros((NE, TOK), F32)
    for k in range(TOP):
        names += (ids[k : k + 1, :] == row_e).astype(F32)
    ti = lax.broadcasted_iota(jnp.int32, (TOK, TOK), 0)
    tj = lax.broadcasted_iota(jnp.int32, (TOK, TOK), 1)
    rank = dot(names.astype(BF), (ti < tj).astype(F32).astype(BF))
    rank = jnp.where(names > 0, rank, -1.0)
    ei = lax.broadcasted_iota(jnp.int32, (1024, NE), 0)
    ej = lax.broadcasted_iota(jnp.int32, (1024, NE), 1)
    spread = (ei // 16 == ej).astype(F32).astype(BF)
    slot = lax.rem(lax.broadcasted_iota(jnp.int32, (1024, TOK), 0), 16).astype(F32)
    gather = (dot(spread, rank.astype(BF)) == slot).astype(F32).astype(BF)

    for k in keep:
        k.wait()

    def wait_back(d, carry):
        t = lax.rem(e + d, NE)
        rows_from(t).wait_recv()
        score_from(t).wait_recv()
        return carry

    lax.fori_loop(1, NE, wait_back, 0)
    tg_ref[...] = dot(gather, back[...].reshape(1024, W), ((0,), (0,))).astype(BF)
    li = lax.broadcasted_iota(jnp.int32, (16, 128), 0)
    lj = lax.broadcasted_iota(jnp.int32, (16, 128), 1)
    mine = (lj == x * 32 + c * 16 + li).astype(F32)
    slots = dot(sback[...].reshape(NE, 128), mine, ((1,), (1,)), lax.Precision.HIGHEST)
    value = jnp.zeros((NE, TOK), F32)
    for j in range(16):
        value += jnp.where(rank == j, slots[:, j : j + 1], 0.0)
    for k in range(TOP):
        sg_ref[k : k + 1, :] = jnp.sum(
            jnp.where(ids[k : k + 1, :] == row_e, value, 0.0), axis=0, keepdims=True
        )

    for k in wout:
        k.wait_recv()
    for k in pend:
        k.wait_send()

    def wait_sent(d, carry):
        t = lax.rem(e + d, NE)
        rows_to(t).wait_send()
        score_to(t).wait_send()
        return carry

    lax.fori_loop(1, NE, wait_sent, 0)


def publish(*refs):
    for i in range(5):
        refs[5 + i][...] = refs[i][...]


def body(
    out_grad, gate_scores, expert_ids, routed_rows, gate_pre, up_pre,
    gate_weight, up_weight, down_weight,
):
    vmem = pl.BlockSpec(memory_space=pltpu.VMEM)
    hbm = pl.BlockSpec(memory_space=pl.ANY)
    dma = pltpu.SemaphoreType.DMA
    outs = pl.pallas_call(
        kernel,
        out_shape=(
            jax.ShapeDtypeStruct((TOK, W), BF),
            jax.ShapeDtypeStruct((TOP, TOK), F32),
            jax.ShapeDtypeStruct((FZ, D), BF),
            jax.ShapeDtypeStruct((FZ, D), BF),
            jax.ShapeDtypeStruct((FZ, D), BF),
        ),
        in_specs=[hbm, vmem, vmem] + [hbm] * 6,
        out_specs=(vmem,) * 5,
        scratch_shapes=[
            pltpu.VMEM((NY, NX, NC, NR, W), BF),
            pltpu.VMEM((2, NZ, FZ, W), BF),
            pltpu.VMEM((NY, NX, 32, W), BF),
            pltpu.VMEM((FZ, 1024), BF),
            pltpu.VMEM((FZ, 1024), BF),
            pltpu.VMEM((FZ, D), BF),
            pltpu.VMEM((NY, 2 * FZ, 128), BF),
            pltpu.VMEM((NY, 128, D), BF),
            pltpu.VMEM((NY, FZ, 128), BF),
            pltpu.VMEM((NY, NZ, 2 * FZ, 128), BF),
            pltpu.VMEM((NZ, NY, 128), F32),
            pltpu.VMEM((NY, 1, 128), F32),
            pltpu.VMEM((2, FF, W), F32),
            pltpu.VMEM((2, NZ, FZ, W), BF),
            pltpu.VMEM((NY, NX, NC, 16, W), BF),
            pltpu.VMEM((NE, 16, W), BF),
            pltpu.VMEM((NE, 1, 128), F32),
            dma((14,)),
            dma((8,)), dma((8,)),
            dma((2, 8)), dma((2, 8)),
            dma((2, 2, 2)), dma((2, 2, 2)),
            dma((2, 5)), dma((2, 5)),
            dma((2, 8, 3)), dma((2, 8, 3)),
            dma((2, 3)), dma((2, 3)),
            dma((2, 4, 5)), dma((2, 4, 5)),
            dma((2, 8)), dma((2, 8)),
            dma((2, 8, 5)), dma((2, 8, 5)),
            dma((8,)), dma((8,)),
            dma((2, 8)), dma((2, 8)),
            dma((NE,)), dma((NE,)),
            dma((NE,)), dma((NE,)),
        ],
        compiler_params=pltpu.CompilerParams(
            collective_id=0, has_side_effects=True, vmem_limit_bytes=56 << 20
        ),
        name="expert_backward",
    )(
        out_grad, expert_ids.T, gate_scores.T, routed_rows.reshape(NX, NY, 32, W),
        gate_pre.reshape(FZ, 1024), up_pre.reshape(FZ, 1024),
        gate_weight.reshape(FZ, D), up_weight.reshape(FZ, D), down_weight.reshape(FZ, D),
    )
    outs = pl.pallas_call(
        publish,
        out_shape=tuple(jax.ShapeDtypeStruct(o.shape, o.dtype) for o in outs),
        in_specs=[vmem] * 5,
        out_specs=(vmem,) * 5,
        name="publish",
    )(*outs)
    token_grad, score_grad, gate_out, up_out, down_out = outs
    return token_grad, score_grad.T, gate_out[None], up_out[None], down_out[None]


def solution(mesh):
    return jax.shard_map(
        body,
        mesh=mesh,
        in_specs=(
            P("exp", "et"), P("exp", None), P("exp", None), P("exp", None, "et"),
            P("exp", "et", None), P("exp", "et", None), P("exp", "et", None),
            P("exp", "et", None), P("exp", "et", None),
        ),
        out_specs=(
            P("exp", "et"), P("exp", None), P("exp", "et", None), P("exp", "et", None),
            P("exp", "et", None),
        ),
        check_vma=False,
    )
```

```python
import functools

import jax
import jax.numpy as jnp
from jax import lax
from jax.experimental import pallas as pl
from jax.experimental.pallas import tpu as pltpu
from jax.sharding import PartitionSpec as P

MESH = pl.DeviceIdType.MESH
BF = jnp.bfloat16
F32 = jnp.float32
NX, NY, NC, NZ, NE = 4, 8, 2, 8, 64
TOK, TOP, W, D, FZ, FF = 64, 8, 256, 2048, 96, 768
META = 512
NR = 528
RA = (0, 320)
RAH = ((0, 160), (160, 160))
RB = (320, 208)
RBH = ((320, 96), (416, 112))
DIRS = (0, 1)
RINGED = (0, 1, -1, 2, -2)


def dot(a, b, dims=((1,), (0,)), precision=None):
    return lax.dot_general(
        a, b, (dims, ((), ())), preferred_element_type=F32, precision=precision
    )


def remote(src, dst, send, recv, target):
    return pltpu.make_async_remote_copy(
        src_ref=src, dst_ref=dst, send_sem=send, recv_sem=recv,
        device_id=target, device_id_type=MESH,
    )


def kernel(
    x_ref, ids_ref, score_ref, rr_ref, gp_hbm, up_hbm, gw_ref, uw_ref, dw_hbm,
    tg_ref, sg_ref, gg_ref, ug_ref, dg_ref,
    tok, wc, rrp, gp_ref, up_ref, dw_ref, gup, row_grad, hsp, gfull, sp, stot, acc, wsend, down, rsend, back, sback,
    lsem, zs, zr, ws, wr, fhs, fhr, ays, ayr, axs, axr, bxs, bxr, bys, byr, prs, prr,
    czs, czr, sps, spr, gs, gr, rs, rr_sem, ss, sr,
):
    e = lax.axis_index("exp")
    z = lax.axis_index("et")
    x = e // 16
    y = lax.rem(e // 2, NY)
    c = lax.rem(e, 2)

    def zz(d):
        return lax.rem(z + d + 16, NZ)

    def yy(d):
        return lax.rem(y + d + 16, NY)

    def xx(d):
        return lax.rem(x + d + 8, NX)

    def at_xy(dx, dy, core):
        return {"exp": (xx(dx) * NY + yy(dy)) * 2 + core}

    barrier = pltpu.get_barrier_semaphore()
    for d in range(1, NZ):
        pl.semaphore_signal(barrier, inc=1, device_id={"et": zz(d)}, device_id_type=MESH)

    near = (at_xy(1, 0, c), at_xy(-1, 0, c), at_xy(0, 1, c), at_xy(0, -1, c), at_xy(0, 0, 1 - c))
    for t in near:
        pl.semaphore_signal(barrier, inc=1, device_id=t, device_id_type=MESH)

    local = [
        pltpu.make_async_copy(x_ref, tok.at[y, x, c, pl.ds(z * TOK, TOK)], lsem.at[0]),
        pltpu.make_async_copy(gp_hbm, gp_ref, lsem.at[1]),
        pltpu.make_async_copy(up_hbm, up_ref, lsem.at[2]),
        pltpu.make_async_copy(dw_hbm, dw_ref, lsem.at[3]),
        pltpu.make_async_copy(gw_ref.at[:, pl.ds(z * W, W)], wc.at[0, z], lsem.at[12]),
        pltpu.make_async_copy(uw_ref.at[:, pl.ds(z * W, W)], wc.at[1, z], lsem.at[13]),
    ]
    for b in range(NY):
        local.append(pltpu.make_async_copy(rr_ref.at[:, b], rrp.at[b], lsem.at[4 + b]))
    for k in local:
        k.start()
    place = lax.rem(x, 2) * 2 + c
    pair_rows = jnp.concatenate(
        [(ids_ref[...] + 1).astype(F32), score_ref[...]], axis=0
    )
    pair_rows = jnp.concatenate([pair_rows] * 4, axis=1)
    lane_block = lax.broadcasted_iota(jnp.int32, (16, W), 1) // TOK
    tok[y, x, c, META : META + 16, :] = jnp.where(lane_block == place, pair_rows, 0.0).astype(BF)
    pl.semaphore_wait(barrier, NZ - 1 + len(near))

    pend = []

    def go(k):
        k.start()
        pend.append(k)

    ztok = {}
    for d in (1, 7, 2, 6, 3, 5, 4):
        k = remote(
            x_ref, tok.at[y, x, c, pl.ds(z * TOK, TOK)], zs.at[d], zr.at[d], {"et": zz(d)}
        )
        go(k)
        ztok[d] = k
    wcols = []

    def send_columns(order):
        for d in order:
            t = zz(d)
            for i, ref in enumerate((gw_ref, uw_ref)):
                k = remote(
                    ref.at[:, pl.ds(t * W, W)], wc.at[i, z], ws.at[i, d], wr.at[i, d], {"et": t}
                )
                go(k)
                wcols.append(k)

    def permute(b, carry):
        q = lax.broadcasted_iota(jnp.int32, (1024, 128), 0)
        p = lax.broadcasted_iota(jnp.int32, (1024, 128), 1)
        sel = (q == (p // 32) * 256 + b * 32 + lax.rem(p, 32)).astype(F32).astype(BF)
        gup[b, 0:FZ] = dot(gp_ref[...], sel).astype(BF)
        gup[b, FZ : 2 * FZ] = dot(up_ref[...], sel).astype(BF)
        return carry

    def sgn(direction):
        return -1 if direction == 0 else 1

    def to_y(direction):
        return at_xy(0, -sgn(direction), c)

    def to_x(direction):
        return at_xy(-sgn(direction), 0, c)

    def a_y(d, s):
        r = RAH[d] if s == 4 else RA
        sl = tok.at[yy(sgn(d) * (s - 1)), x, c, pl.ds(*r)]
        if s == 1:
            return remote(sl, sl, fhs.at[0, d, 0], fhr.at[0, d, 0], to_y(d))
        return remote(sl, sl, ays.at[d, s], ayr.at[d, s], to_y(d))

    def a_x(d, g, s):
        r = RAH[d] if s == 2 else RA
        sl = tok.at[yy(g), xx(sgn(d) * (s - 1)), c, pl.ds(*r)]
        if g == 0 and s == 1:
            return remote(sl, sl, fhs.at[1, d, 0], fhr.at[1, d, 0], to_x(d))
        return remote(sl, sl, axs.at[d, g % 8, s], axr.at[d, g % 8, s], to_x(d))

    def b_x(d, s):
        r = RBH[d] if s == 2 else RB
        sl = tok.at[y, xx(sgn(d) * (s - 1)), c, pl.ds(*r)]
        if s == 1:
            return remote(sl, sl, fhs.at[1, d, 1], fhr.at[1, d, 1], to_x(d))
        return remote(sl, sl, bxs.at[d, s], bxr.at[d, s], to_x(d))

    def b_y(d, q, s):
        r = RBH[d] if s == 4 else RB
        sl = tok.at[yy(sgn(d) * (s - 1)), xx(q), c, pl.ds(*r)]
        if q == 0 and s == 1:
            return remote(sl, sl, fhs.at[0, d, 1], fhr.at[0, d, 1], to_y(d))
        return remote(sl, sl, bys.at[d, q % 4, s], byr.at[d, q % 4, s], to_y(d))

    def pair(g, i):
        sl = tok.at[yy(g), :, c, pl.ds(*(RA, RB)[i])]
        return remote(sl, sl, prs.at[i, g % 8], prr.at[i, g % 8], at_xy(0, 0, 1 - c))

    def c_z(d, g, s):
        held = 2 if s == 4 and g not in RINGED else s - 1
        sl = gfull.at[yy(g), zz(sgn(d) * held)]
        if s == 4:
            sl = sl.at[pl.ds(d * FZ, FZ)]
        far = s - held
        return remote(
            sl, sl, czs.at[d, g % 8, s], czr.at[d, g % 8, s], {"et": zz(-sgn(d) * far)}
        )

    def compute(g):
        for i in range(2):
            pair(g, i).wait_recv()
        b = yy(g)
        lane = lax.broadcasted_iota(jnp.int32, (1, W), 1)
        ui = lax.broadcasted_iota(jnp.int32, (W, W), 0)
        uj = lax.broadcasted_iota(jnp.int32, (W, W), 1)
        upper = ((ui < uj) & (ui // TOK == uj // TOK)).astype(F32).astype(BF)
        srow = jnp.zeros((8, 128), F32)
        picks = []
        for h in range(2):
            mt = tok[b, 2 * h : 2 * h + 2, :, META : META + 16, :].reshape(4, 16, W).astype(F32)
            hit = (mt[:, 0:8, :] == (e + 1).astype(F32)).astype(F32)
            m = jnp.sum(hit, axis=(0, 1))[None]
            sv = jnp.sum(hit * mt[:, 8:16, :], axis=(0, 1))[None]
            rank = dot(jnp.broadcast_to(m, (8, W)).astype(BF), upper)[0:1]
            want = jnp.where(m > 0, rank.astype(jnp.int32) + 16 * (lane // TOK) + 64 * h, -1)
            slot = lax.broadcasted_iota(jnp.int32, (128, W), 0)
            pick = (slot == want).astype(F32).astype(BF)
            picks.append(pick)
            srow += dot(jnp.broadcast_to(sv, (8, W)).astype(BF), pick, ((1,), (1,)))
        srow = srow[0:1]
        hr = jnp.zeros((FZ, 128), F32)
        for f in range(NZ):
            rows = jnp.zeros((128, W), F32)
            for h in range(2):
                part = tok[b, 2 * h : 2 * h + 2, :, f * TOK : (f + 1) * TOK, :].reshape(W, W)
                rows += dot(picks[h], part)
            rows = rows.astype(BF)
            row_grad[b, :, f * W : (f + 1) * W] = rows
            hr += dot(dw_ref[:, f * W : (f + 1) * W], rows, ((1,), (1,)))
        gate = gup[b, 0:FZ].astype(F32)
        up = gup[b, FZ : 2 * FZ].astype(F32)
        sig = jax.nn.sigmoid(gate)
        silu = gate * sig
        hidden = (silu * up).astype(BF).astype(F32)
        sp[z, pl.ds(b, 1), :] = jnp.sum(hidden * hr, axis=0, keepdims=True)
        hg = srow * hr
        gfull[b, z, 0:FZ] = (hg * up * sig * (1.0 + gate * (1.0 - sig))).astype(BF)
        gfull[b, z, FZ : 2 * FZ] = (hg * silu).astype(BF)
        hsp[b] = (hidden * srow).astype(BF)
        for d in DIRS:
            go(c_z(d, g, 1))

    def step(g):
        for d in DIRS:
            c_z(d, g, 1).wait_recv()
            go(c_z(d, g, 2))

    def relay(g):
        for d in DIRS:
            c_z(d, g, 2).wait_recv()
            for s in (3,) if g in RINGED else (3, 4):
                go(c_z(d, g, s))

    def last(g):
        for d in DIRS:
            c_z(d, g, 3).wait_recv()
            go(c_z(d, g, 4))

    def collect(g):
        for s in (4,) if g in RINGED else (3, 4):
            for d in DIRS:
                c_z(d, g, s).wait_recv()

    def weights_part(g, first):
        b = yy(g)
        for i in range(2):
            part = dot(gfull[b, :, i * FZ : (i + 1) * FZ, :].reshape(FF, 128), rrp[b].reshape(128, W))
            if first:
                acc[i] = part
            else:
                acc[i] += part

    def rows_part(g):
        b = yy(g)
        out = dot(gfull[b, :, 0:FZ, :].reshape(FF, 128), wc[0].reshape(FF, W), ((0,), (0,)))
        out += dot(
            gfull[b, :, FZ : 2 * FZ, :].reshape(FF, 128), wc[1].reshape(FF, W), ((0,), (0,))
        )
        rsend[b] = out.astype(BF).reshape(NX, NC, 16, W)

    def piece(d, axis, src, rows, part):
        dst = tok.at[y, x, c, rows]
        return remote(
            dst if src is None else src, dst, fhs.at[axis, d, part], fhr.at[axis, d, part],
            (to_y, to_x)[axis](d),
        )

    def send_piece(src, rows, part):
        for axis in (1, 0):
            for d in DIRS:
                piece(d, axis, src, rows, part).start()

    send_piece(None, pl.ds(META, 16), 1)
    send_piece(x_ref, pl.ds(z * TOK, TOK), z // 5)
    for d in (1, 7, 2, 6, 3, 5, 4):
        ztok[d].wait_recv()
        f = zz(-d)
        send_piece(None, pl.ds(f * TOK, TOK), f // 5)
    for d in DIRS:
        pend.extend([a_y(d, 1), a_x(d, 0, 1), b_x(d, 1), b_y(d, 0, 1)])
    send_columns((1, 7, 2, 6, 3, 5, 4))
    for k in local:
        k.wait()
    lax.fori_loop(0, NY, permute, 0)

    order = (0, 1, -1, 2, -2, 3, -3, 4)
    done = []
    unsent = []

    def ax0(g):
        for d in DIRS:
            go(a_x(d, g, 1))

    def ax1(g):
        for d in DIRS:
            a_x(d, g, 1).wait_recv()
            go(a_x(d, g, 2))

    def ay(k):
        for d in DIRS:
            a_y(d, k).wait_recv()
            if k < 4:
                go(a_y(d, k + 1))

    def bx1():
        for d in DIRS:
            b_x(d, 1).wait_recv()
            go(b_x(d, 2))
        for q in (-1, 1):
            for d in DIRS:
                go(b_y(d, q, 1))

    def bx2():
        for d in DIRS:
            b_x(d, 2).wait_recv()
        for d in DIRS:
            go(b_y(d, 2, 1))

    def by(q, k):
        for d in DIRS:
            b_y(d, q, k).wait_recv()
            if k < 4:
                go(b_y(d, q, k + 1))

    def pb(g):
        go(pair(g, 1))

    def fin(g):
        for d in DIRS:
            a_x(d, g, 2).wait_recv()
        go(pair(g, 0))

    def take(g):
        collect(g)
        weights_part(g, not done)
        if not done:
            for k in wcols:
                k.wait_recv()
        rows_part(g)
        done.append(g)
        unsent.append(g)

    comp = compute
    plan = [
        (bx1,), (ay, 1), (ax0, 1), (ax0, -1), (bx2,), (pb, 0), (ax1, 0), (ay, 2), (ax0, 2),
        (ax0, -2), (by, 0, 1), (by, 1, 1), (fin, 0), (ax1, 1), (ay, 3), (by, -1, 1), (by, 2, 1),
        (pb, 1), (pb, -1), (comp, 0), (ax1, -1), (ax0, 3), (ax0, -3), (by, 0, 2), (fin, 1),
        (ay, 4), (by, 1, 2), (ax1, 2), (comp, 1), (step, 0), (by, -1, 2), (ax0, 4), (fin, -1),
        (by, 2, 2), (pb, 2), (pb, -2), (comp, -1), (step, 1), (ax1, -2), (by, 0, 3), (fin, 2),
        (by, 1, 3), (ax1, 3), (comp, 2), (relay, 0), (step, -1), (by, -1, 3), (fin, -2),
        (by, 2, 3), (pb, 3), (pb, -3), (comp, -2), (last, 0), (relay, 1), (step, 2), (ax1, -3),
        (by, 0, 4), (fin, 3), (ax1, 4), (by, 1, 4), (comp, 3), (last, 1), (relay, -1), (step, -2),
        (by, -1, 4), (by, 2, 4), (pb, 4), (fin, -3), (comp, -3), (take, 0), (last, -1),
        (relay, 2), (step, 3), (fin, 4), (comp, 4), (take, 1), (last, 2), (relay, -2), (step, -3),
    ]
    for event, *given in plan:
        event(*given)

    def target_rows(t):
        src = rsend.at[lax.rem(t // 2, NY), t // 16, lax.rem(t, 2)]
        return src

    def rows_to(t):
        return remote(target_rows(t), back.at[e], rs.at[t], rr_sem.at[e], {"exp": t})

    def rows_from(t):
        return remote(target_rows(e), back.at[t], rs.at[t], rr_sem.at[t], {"exp": t})

    def score_to(t):
        return remote(
            stot.at[lax.rem(t // 2, NY)], sback.at[e], ss.at[t], sr.at[e], {"exp": t}
        )

    def score_from(t):
        return remote(stot.at[y], sback.at[t], ss.at[t], sr.at[t], {"exp": t})

    def send_rows(g):
        for dx in (0, 1, -1, 2):
            for core in range(2):
                if g == 0 and dx == 0:
                    if core == 0:
                        rows_to(at_xy(0, 0, 1 - c)["exp"]).start()
                    continue
                rows_to(at_xy(dx, g, core)["exp"]).start()

    for d in range(1, NZ):
        go(remote(sp.at[z], sp.at[z], sps.at[d], spr.at[d], {"et": zz(d)}))
    step(4)
    if unsent:
        send_rows(unsent.pop(0))
    last(-2)
    if unsent:
        send_rows(unsent.pop(0))
    relay(3)
    if unsent:
        send_rows(unsent.pop(0))
    relay(-3)
    if unsent:
        send_rows(unsent.pop(0))
    relay(4)
    if unsent:
        send_rows(unsent.pop(0))
    take(-1)
    send_rows(unsent.pop(0))
    take(2)
    send_rows(unsent.pop(0))
    take(-2)
    send_rows(unsent.pop(0))
    take(3)
    send_rows(unsent.pop(0))
    take(-3)
    send_rows(unsent.pop(0))
    take(4)
    for i in range(2):
        wsend[i] = acc[i].astype(BF).reshape(NZ, FZ, W)
    wout = []
    for d in (4, 3, 5, 2, 6, 1, 7):
        t = zz(d)
        for i, ref in enumerate((gg_ref, ug_ref)):
            k = remote(
                wsend.at[i, t], ref.at[:, pl.ds(z * W, W)], gs.at[i, d], gr.at[i, d], {"et": t}
            )
            go(k)
            wout.append(k)
    for g in unsent:
        send_rows(g)
    for d in range(1, NZ):
        remote(sp.at[z], sp.at[z], sps.at[d], spr.at[d], {"et": zz(d)}).wait_recv()
    total = sp[0]
    for i in range(1, NZ):
        total = total + sp[i]
    stot[...] = total.reshape(NY, 1, 128)

    def send_scores(d, carry):
        score_to(lax.rem(e + d, NE)).start()
        return carry

    lax.fori_loop(1, NE, send_scores, 0)
    keep = [
        pltpu.make_async_copy(rsend.at[y, x, c], back.at[e], lsem.at[0]),
        pltpu.make_async_copy(stot.at[y], sback.at[e], lsem.at[1]),
        pltpu.make_async_copy(wsend.at[0, z], gg_ref.at[:, pl.ds(z * W, W)], lsem.at[2]),
        pltpu.make_async_copy(wsend.at[1, z], ug_ref.at[:, pl.ds(z * W, W)], lsem.at[3]),
    ]
    for k in keep:
        k.start()

    hs = jnp.concatenate([hsp[b] for b in range(NY)], axis=1)
    for f in range(NZ):
        rows = row_grad[:, :, f * W : (f + 1) * W].reshape(1024, W)
        down[:, f * W : (f + 1) * W] = dot(hs, rows).astype(BF)
    out_down = pltpu.make_async_copy(down, dg_ref, lsem.at[4])
    out_down.start()

    ids = ids_ref[...]
    row_e = lax.broadcasted_iota(jnp.int32, (NE, TOK), 0)
    names = jnp.zeros((NE, TOK), F32)
    for k in range(TOP):
        names += (ids[k : k + 1, :] == row_e).astype(F32)
    ti = lax.broadcasted_iota(jnp.int32, (TOK, TOK), 0)
    tj = lax.broadcasted_iota(jnp.int32, (TOK, TOK), 1)
    rank = dot(names.astype(BF), (ti < tj).astype(F32).astype(BF))
    rank = jnp.where(names > 0, rank, -1.0)
    ei = lax.broadcasted_iota(jnp.int32, (1024, NE), 0)
    ej = lax.broadcasted_iota(jnp.int32, (1024, NE), 1)
    spread = (ei // 16 == ej).astype(F32).astype(BF)
    slot = lax.rem(lax.broadcasted_iota(jnp.int32, (1024, TOK), 0), 16).astype(F32)
    gather = (dot(spread, rank.astype(BF)) == slot).astype(F32).astype(BF)

    for k in keep:
        k.wait()

    def wait_back(d, carry):
        t = lax.rem(e + d, NE)
        rows_from(t).wait_recv()
        score_from(t).wait_recv()
        return carry

    lax.fori_loop(1, NE, wait_back, 0)
    tg_ref[...] = dot(gather, back[...].reshape(1024, W), ((0,), (0,))).astype(BF)
    li = lax.broadcasted_iota(jnp.int32, (16, 128), 0)
    lj = lax.broadcasted_iota(jnp.int32, (16, 128), 1)
    mine = (lj == x * 32 + c * 16 + li).astype(F32)
    slots = dot(sback[...].reshape(NE, 128), mine, ((1,), (1,)), lax.Precision.HIGHEST)
    value = jnp.zeros((NE, TOK), F32)
    for j in range(16):
        value += jnp.where(rank == j, slots[:, j : j + 1], 0.0)
    for k in range(TOP):
        sg_ref[k : k + 1, :] = jnp.sum(
            jnp.where(ids[k : k + 1, :] == row_e, value, 0.0), axis=0, keepdims=True
        )

    out_down.wait()
    for k in wout:
        k.wait_recv()
    for k in pend:
        k.wait_send()

    def wait_sent(d, carry):
        t = lax.rem(e + d, NE)
        rows_to(t).wait_send()
        score_to(t).wait_send()
        return carry

    lax.fori_loop(1, NE, wait_sent, 0)


def publish(*refs):
    for i in range(5):
        refs[5 + i][...] = refs[i][...]


def body(
    out_grad, gate_scores, expert_ids, routed_rows, gate_pre, up_pre,
    gate_weight, up_weight, down_weight,
):
    vmem = pl.BlockSpec(memory_space=pltpu.VMEM)
    hbm = pl.BlockSpec(memory_space=pl.ANY)
    dma = pltpu.SemaphoreType.DMA
    outs = pl.pallas_call(
        kernel,
        out_shape=(
            jax.ShapeDtypeStruct((TOK, W), BF),
            jax.ShapeDtypeStruct((TOP, TOK), F32),
            jax.ShapeDtypeStruct((FZ, D), BF),
            jax.ShapeDtypeStruct((FZ, D), BF),
            jax.ShapeDtypeStruct((FZ, D), BF),
        ),
        in_specs=[hbm, vmem, vmem] + [hbm] * 6,
        out_specs=(vmem, vmem, hbm, hbm, hbm),
        scratch_shapes=[
            pltpu.VMEM((NY, NX, NC, NR, W), BF),
            pltpu.VMEM((2, NZ, FZ, W), BF),
            pltpu.VMEM((NY, NX, 32, W), BF),
            pltpu.VMEM((FZ, 1024), BF),
            pltpu.VMEM((FZ, 1024), BF),
            pltpu.VMEM((FZ, D), BF),
            pltpu.VMEM((NY, 2 * FZ, 128), BF),
            pltpu.VMEM((NY, 128, D), BF),
            pltpu.VMEM((NY, FZ, 128), BF),
            pltpu.VMEM((NY, NZ, 2 * FZ, 128), BF),
            pltpu.VMEM((NZ, NY, 128), F32),
            pltpu.VMEM((NY, 1, 128), F32),
            pltpu.VMEM((2, FF, W), F32),
            pltpu.VMEM((2, NZ, FZ, W), BF),
            pltpu.VMEM((FZ, D), BF),
            pltpu.VMEM((NY, NX, NC, 16, W), BF),
            pltpu.VMEM((NE, 16, W), BF),
            pltpu.VMEM((NE, 1, 128), F32),
            dma((14,)),
            dma((8,)), dma((8,)),
            dma((2, 8)), dma((2, 8)),
            dma((2, 2, 2)), dma((2, 2, 2)),
            dma((2, 5)), dma((2, 5)),
            dma((2, 8, 3)), dma((2, 8, 3)),
            dma((2, 3)), dma((2, 3)),
            dma((2, 4, 5)), dma((2, 4, 5)),
            dma((2, 8)), dma((2, 8)),
            dma((2, 8, 5)), dma((2, 8, 5)),
            dma((8,)), dma((8,)),
            dma((2, 8)), dma((2, 8)),
            dma((NE,)), dma((NE,)),
            dma((NE,)), dma((NE,)),
        ],
        compiler_params=pltpu.CompilerParams(
            collective_id=0, has_side_effects=True, vmem_limit_bytes=56 << 20
        ),
        name="expert_backward",
    )(
        out_grad, expert_ids.T, gate_scores.T, routed_rows.reshape(NX, NY, 32, W),
        gate_pre.reshape(FZ, 1024), up_pre.reshape(FZ, 1024),
        gate_weight.reshape(FZ, D), up_weight.reshape(FZ, D), down_weight.reshape(FZ, D),
    )
    outs = pl.pallas_call(
        publish,
        out_shape=tuple(jax.ShapeDtypeStruct(o.shape, o.dtype) for o in outs),
        in_specs=[vmem] * 5,
        out_specs=(vmem,) * 5,
        name="publish",
    )(*outs)
    token_grad, score_grad, gate_out, up_out, down_out = outs
    return token_grad, score_grad.T, gate_out[None], up_out[None], down_out[None]


def solution(mesh):
    return jax.shard_map(
        body,
        mesh=mesh,
        in_specs=(
            P("exp", "et"), P("exp", None), P("exp", None), P("exp", None, "et"),
            P("exp", "et", None), P("exp", "et", None), P("exp", "et", None),
            P("exp", "et", None), P("exp", "et", None),
        ),
        out_specs=(
            P("exp", "et"), P("exp", None), P("exp", "et", None), P("exp", "et", None),
            P("exp", "et", None),
        ),
        check_vma=False,
    )
```

```python
import functools

import jax
import jax.numpy as jnp
from jax import lax
from jax.experimental import pallas as pl
from jax.experimental.pallas import tpu as pltpu
from jax.sharding import PartitionSpec as P

MESH = pl.DeviceIdType.MESH
BF = jnp.bfloat16
F32 = jnp.float32
NX, NY, NC, NZ, NE = 4, 8, 2, 8, 64
TOK, TOP, W, D, FZ, FF = 64, 8, 256, 2048, 96, 768
META = 512
NR = 528
RA = (0, 320)
RAH = ((0, 160), (160, 160))
RB = (320, 208)
RBH = ((320, 96), (416, 112))
DIRS = (0, 1)
RINGED = (0, 1, -1, 2, -2, 3)


def dot(a, b, dims=((1,), (0,)), precision=None):
    return lax.dot_general(
        a, b, (dims, ((), ())), preferred_element_type=F32, precision=precision
    )


def remote(src, dst, send, recv, target):
    return pltpu.make_async_remote_copy(
        src_ref=src, dst_ref=dst, send_sem=send, recv_sem=recv,
        device_id=target, device_id_type=MESH,
    )


def kernel(
    x_ref, ids_ref, score_ref, rr_ref, gp_hbm, up_hbm, gw_ref, uw_ref, dw_hbm,
    tg_ref, sg_ref, gg_ref, ug_ref, dg_ref,
    tok, wc, rrp, gp_ref, up_ref, dw_ref, gup, row_grad, hsp, gfull, sp, stot, acc, wsend, down, rsend, back, sback,
    lsem, zs, zr, ws, wr, fhs, fhr, ays, ayr, axs, axr, bxs, bxr, bys, byr, prs, prr,
    czs, czr, sps, spr, gs, gr, rs, rr_sem, ss, sr,
):
    e = lax.axis_index("exp")
    z = lax.axis_index("et")
    x = e // 16
    y = lax.rem(e // 2, NY)
    c = lax.rem(e, 2)

    def zz(d):
        return lax.rem(z + d + 16, NZ)

    def yy(d):
        return lax.rem(y + d + 16, NY)

    def xx(d):
        return lax.rem(x + d + 8, NX)

    def at_xy(dx, dy, core):
        return {"exp": (xx(dx) * NY + yy(dy)) * 2 + core}

    barrier = pltpu.get_barrier_semaphore()
    for d in range(1, NZ):
        pl.semaphore_signal(barrier, inc=1, device_id={"et": zz(d)}, device_id_type=MESH)

    near = (at_xy(1, 0, c), at_xy(-1, 0, c), at_xy(0, 1, c), at_xy(0, -1, c), at_xy(0, 0, 1 - c))
    for t in near:
        pl.semaphore_signal(barrier, inc=1, device_id=t, device_id_type=MESH)

    local = [
        pltpu.make_async_copy(x_ref, tok.at[y, x, c, pl.ds(z * TOK, TOK)], lsem.at[0]),
        pltpu.make_async_copy(gp_hbm, gp_ref, lsem.at[1]),
        pltpu.make_async_copy(up_hbm, up_ref, lsem.at[2]),
        pltpu.make_async_copy(dw_hbm, dw_ref, lsem.at[3]),
        pltpu.make_async_copy(gw_ref.at[:, pl.ds(z * W, W)], wc.at[0, z], lsem.at[12]),
        pltpu.make_async_copy(uw_ref.at[:, pl.ds(z * W, W)], wc.at[1, z], lsem.at[13]),
    ]
    for b in range(NY):
        local.append(pltpu.make_async_copy(rr_ref.at[:, b], rrp.at[b], lsem.at[4 + b]))
    for k in local:
        k.start()
    place = lax.rem(x, 2) * 2 + c
    pair_rows = jnp.concatenate(
        [(ids_ref[...] + 1).astype(F32), score_ref[...]], axis=0
    )
    pair_rows = jnp.concatenate([pair_rows] * 4, axis=1)
    lane_block = lax.broadcasted_iota(jnp.int32, (16, W), 1) // TOK
    tok[y, x, c, META : META + 16, :] = jnp.where(lane_block == place, pair_rows, 0.0).astype(BF)
    pl.semaphore_wait(barrier, NZ - 1 + len(near))

    pend = []

    def go(k):
        k.start()
        pend.append(k)

    ztok = {}
    for d in (1, 7, 2, 6, 3, 5, 4):
        k = remote(
            x_ref, tok.at[y, x, c, pl.ds(z * TOK, TOK)], zs.at[d], zr.at[d], {"et": zz(d)}
        )
        go(k)
        ztok[d] = k
    wcols = []

    def send_columns(order):
        for d in order:
            t = zz(d)
            for i, ref in enumerate((gw_ref, uw_ref)):
                k = remote(
                    ref.at[:, pl.ds(t * W, W)], wc.at[i, z], ws.at[i, d], wr.at[i, d], {"et": t}
                )
                go(k)
                wcols.append(k)

    def permute(b, carry):
        q = lax.broadcasted_iota(jnp.int32, (1024, 128), 0)
        p = lax.broadcasted_iota(jnp.int32, (1024, 128), 1)
        sel = (q == (p // 32) * 256 + b * 32 + lax.rem(p, 32)).astype(F32).astype(BF)
        gup[b, 0:FZ] = dot(gp_ref[...], sel).astype(BF)
        gup[b, FZ : 2 * FZ] = dot(up_ref[...], sel).astype(BF)
        return carry

    def sgn(direction):
        return -1 if direction == 0 else 1

    def to_y(direction):
        return at_xy(0, -sgn(direction), c)

    def to_x(direction):
        return at_xy(-sgn(direction), 0, c)

    def a_y(d, s):
        r = RAH[d] if s == 4 else RA
        sl = tok.at[yy(sgn(d) * (s - 1)), x, c, pl.ds(*r)]
        if s == 1:
            return remote(sl, sl, fhs.at[0, d, 0], fhr.at[0, d, 0], to_y(d))
        return remote(sl, sl, ays.at[d, s], ayr.at[d, s], to_y(d))

    def a_x(d, g, s):
        r = RAH[d] if s == 2 else RA
        sl = tok.at[yy(g), xx(sgn(d) * (s - 1)), c, pl.ds(*r)]
        if g == 0 and s == 1:
            return remote(sl, sl, fhs.at[1, d, 0], fhr.at[1, d, 0], to_x(d))
        return remote(sl, sl, axs.at[d, g % 8, s], axr.at[d, g % 8, s], to_x(d))

    def b_x(d, s):
        r = RBH[d] if s == 2 else RB
        sl = tok.at[y, xx(sgn(d) * (s - 1)), c, pl.ds(*r)]
        if s == 1:
            return remote(sl, sl, fhs.at[1, d, 1], fhr.at[1, d, 1], to_x(d))
        return remote(sl, sl, bxs.at[d, s], bxr.at[d, s], to_x(d))

    def b_y(d, q, s):
        r = RBH[d] if s == 4 else RB
        sl = tok.at[yy(sgn(d) * (s - 1)), xx(q), c, pl.ds(*r)]
        if q == 0 and s == 1:
            return remote(sl, sl, fhs.at[0, d, 1], fhr.at[0, d, 1], to_y(d))
        return remote(sl, sl, bys.at[d, q % 4, s], byr.at[d, q % 4, s], to_y(d))

    def pair(g, i):
        sl = tok.at[yy(g), :, c, pl.ds(*(RA, RB)[i])]
        return remote(sl, sl, prs.at[i, g % 8], prr.at[i, g % 8], at_xy(0, 0, 1 - c))

    def c_z(d, g, s):
        held = 2 if s == 4 and g not in RINGED else s - 1
        sl = gfull.at[yy(g), zz(sgn(d) * held)]
        if s == 4:
            sl = sl.at[pl.ds(d * FZ, FZ)]
        far = s - held
        return remote(
            sl, sl, czs.at[d, g % 8, s], czr.at[d, g % 8, s], {"et": zz(-sgn(d) * far)}
        )

    def compute(g):
        for i in range(2):
            pair(g, i).wait_recv()
        b = yy(g)
        lane = lax.broadcasted_iota(jnp.int32, (1, W), 1)
        ui = lax.broadcasted_iota(jnp.int32, (W, W), 0)
        uj = lax.broadcasted_iota(jnp.int32, (W, W), 1)
        upper = ((ui < uj) & (ui // TOK == uj // TOK)).astype(F32).astype(BF)
        srow = jnp.zeros((8, 128), F32)
        picks = []
        for h in range(2):
            mt = tok[b, 2 * h : 2 * h + 2, :, META : META + 16, :].reshape(4, 16, W).astype(F32)
            hit = (mt[:, 0:8, :] == (e + 1).astype(F32)).astype(F32)
            m = jnp.sum(hit, axis=(0, 1))[None]
            sv = jnp.sum(hit * mt[:, 8:16, :], axis=(0, 1))[None]
            rank = dot(jnp.broadcast_to(m, (8, W)).astype(BF), upper)[0:1]
            want = jnp.where(m > 0, rank.astype(jnp.int32) + 16 * (lane // TOK) + 64 * h, -1)
            slot = lax.broadcasted_iota(jnp.int32, (128, W), 0)
            pick = (slot == want).astype(F32).astype(BF)
            picks.append(pick)
            srow += dot(jnp.broadcast_to(sv, (8, W)).astype(BF), pick, ((1,), (1,)))
        srow = srow[0:1]
        hr = jnp.zeros((FZ, 128), F32)
        for f in range(NZ):
            rows = jnp.zeros((128, W), F32)
            for h in range(2):
                part = tok[b, 2 * h : 2 * h + 2, :, f * TOK : (f + 1) * TOK, :].reshape(W, W)
                rows += dot(picks[h], part)
            rows = rows.astype(BF)
            row_grad[b, :, f * W : (f + 1) * W] = rows
            hr += dot(dw_ref[:, f * W : (f + 1) * W], rows, ((1,), (1,)))
        gate = gup[b, 0:FZ].astype(F32)
        up = gup[b, FZ : 2 * FZ].astype(F32)
        sig = jax.nn.sigmoid(gate)
        silu = gate * sig
        hidden = (silu * up).astype(BF).astype(F32)
        sp[z, pl.ds(b, 1), :] = jnp.sum(hidden * hr, axis=0, keepdims=True)
        hg = srow * hr
        gfull[b, z, 0:FZ] = (hg * up * sig * (1.0 + gate * (1.0 - sig))).astype(BF)
        gfull[b, z, FZ : 2 * FZ] = (hg * silu).astype(BF)
        hsp[b] = (hidden * srow).astype(BF)
        for d in DIRS:
            go(c_z(d, g, 1))

    def step(g):
        for d in DIRS:
            c_z(d, g, 1).wait_recv()
            go(c_z(d, g, 2))

    def relay(g):
        for d in DIRS:
            c_z(d, g, 2).wait_recv()
            for s in (3,) if g in RINGED else (3, 4):
                go(c_z(d, g, s))

    def last(g):
        for d in DIRS:
            c_z(d, g, 3).wait_recv()
            go(c_z(d, g, 4))

    def collect(g):
        for s in (4,) if g in RINGED else (3, 4):
            for d in DIRS:
                c_z(d, g, s).wait_recv()

    def weights_part(g, first):
        b = yy(g)
        for i in range(2):
            part = dot(gfull[b, :, i * FZ : (i + 1) * FZ, :].reshape(FF, 128), rrp[b].reshape(128, W))
            if first:
                acc[i] = part
            else:
                acc[i] += part

    def rows_part(g):
        b = yy(g)
        out = dot(gfull[b, :, 0:FZ, :].reshape(FF, 128), wc[0].reshape(FF, W), ((0,), (0,)))
        out += dot(
            gfull[b, :, FZ : 2 * FZ, :].reshape(FF, 128), wc[1].reshape(FF, W), ((0,), (0,))
        )
        rsend[b] = out.astype(BF).reshape(NX, NC, 16, W)

    def piece(d, axis, src, rows, part):
        dst = tok.at[y, x, c, rows]
        return remote(
            dst if src is None else src, dst, fhs.at[axis, d, part], fhr.at[axis, d, part],
            (to_y, to_x)[axis](d),
        )

    def send_piece(src, rows, part):
        for axis in (1, 0):
            for d in DIRS:
                piece(d, axis, src, rows, part).start()

    send_piece(None, pl.ds(META, 16), 1)
    send_piece(x_ref, pl.ds(z * TOK, TOK), z // 5)
    for d in (1, 7, 2, 6, 3, 5, 4):
        ztok[d].wait_recv()
        f = zz(-d)
        send_piece(None, pl.ds(f * TOK, TOK), f // 5)
    for d in DIRS:
        pend.extend([a_y(d, 1), a_x(d, 0, 1), b_x(d, 1), b_y(d, 0, 1)])
    send_columns((1, 7, 2, 6, 3, 5, 4))
    for k in local:
        k.wait()
    lax.fori_loop(0, NY, permute, 0)

    order = (0, 1, -1, 2, -2, 3, -3, 4)
    done = []
    unsent = []

    def ax0(g):
        for d in DIRS:
            go(a_x(d, g, 1))

    def ax1(g):
        for d in DIRS:
            a_x(d, g, 1).wait_recv()
            go(a_x(d, g, 2))

    def ay(k):
        for d in DIRS:
            a_y(d, k).wait_recv()
            if k < 4:
                go(a_y(d, k + 1))

    def bx1():
        for d in DIRS:
            b_x(d, 1).wait_recv()
            go(b_x(d, 2))
        for q in (-1, 1):
            for d in DIRS:
                go(b_y(d, q, 1))

    def bx2():
        for d in DIRS:
            b_x(d, 2).wait_recv()
        for d in DIRS:
            go(b_y(d, 2, 1))

    def by(q, k):
        for d in DIRS:
            b_y(d, q, k).wait_recv()
            if k < 4:
                go(b_y(d, q, k + 1))

    def pb(g):
        go(pair(g, 1))

    def fin(g):
        for d in DIRS:
            a_x(d, g, 2).wait_recv()
        go(pair(g, 0))

    def take(g):
        collect(g)
        weights_part(g, not done)
        if not done:
            for k in wcols:
                k.wait_recv()
        rows_part(g)
        done.append(g)
        unsent.append(g)

    comp = compute
    plan = [
        (bx1,), (ay, 1), (ax0, 1), (ax0, -1), (bx2,), (pb, 0), (ax1, 0), (ay, 2), (ax0, 2),
        (ax0, -2), (by, 0, 1), (by, 1, 1), (fin, 0), (ax1, 1), (ay, 3), (by, -1, 1), (by, 2, 1),
        (pb, 1), (pb, -1), (comp, 0), (ax1, -1), (ax0, 3), (ax0, -3), (by, 0, 2), (fin, 1),
        (ay, 4), (by, 1, 2), (ax1, 2), (comp, 1), (step, 0), (by, -1, 2), (ax0, 4), (fin, -1),
        (by, 2, 2), (pb, 2), (pb, -2), (comp, -1), (step, 1), (ax1, -2), (by, 0, 3), (fin, 2),
        (by, 1, 3), (ax1, 3), (comp, 2), (relay, 0), (step, -1), (by, -1, 3), (fin, -2),
        (by, 2, 3), (pb, 3), (pb, -3), (comp, -2), (last, 0), (relay, 1), (step, 2), (ax1, -3),
        (by, 0, 4), (fin, 3), (ax1, 4), (by, 1, 4), (comp, 3), (last, 1), (relay, -1), (step, -2),
        (by, -1, 4), (by, 2, 4), (pb, 4), (fin, -3), (comp, -3), (take, 0), (last, -1),
        (relay, 2), (step, 3), (fin, 4), (comp, 4), (take, 1), (last, 2), (relay, -2), (step, -3),
    ]
    for event, *given in plan:
        event(*given)

    def target_rows(t):
        src = rsend.at[lax.rem(t // 2, NY), t // 16, lax.rem(t, 2)]
        return src

    def rows_to(t):
        return remote(target_rows(t), back.at[e], rs.at[t], rr_sem.at[e], {"exp": t})

    def rows_from(t):
        return remote(target_rows(e), back.at[t], rs.at[t], rr_sem.at[t], {"exp": t})

    def score_to(t):
        return remote(
            stot.at[lax.rem(t // 2, NY)], sback.at[e], ss.at[t], sr.at[e], {"exp": t}
        )

    def score_from(t):
        return remote(stot.at[y], sback.at[t], ss.at[t], sr.at[t], {"exp": t})

    def send_rows(g):
        for dx in (0, 1, -1, 2):
            for core in range(2):
                if g == 0 and dx == 0:
                    if core == 0:
                        rows_to(at_xy(0, 0, 1 - c)["exp"]).start()
                    continue
                rows_to(at_xy(dx, g, core)["exp"]).start()

    for d in range(1, NZ):
        go(remote(sp.at[z], sp.at[z], sps.at[d], spr.at[d], {"et": zz(d)}))
    step(4)
    if unsent:
        send_rows(unsent.pop(0))
    relay(3)
    if unsent:
        send_rows(unsent.pop(0))
    relay(-3)
    if unsent:
        send_rows(unsent.pop(0))
    relay(4)
    if unsent:
        send_rows(unsent.pop(0))
    last(-2)
    if unsent:
        send_rows(unsent.pop(0))
    last(3)
    if unsent:
        send_rows(unsent.pop(0))
    take(-1)
    send_rows(unsent.pop(0))
    take(2)
    send_rows(unsent.pop(0))
    take(-2)
    send_rows(unsent.pop(0))
    take(3)
    send_rows(unsent.pop(0))
    take(-3)
    send_rows(unsent.pop(0))
    take(4)
    for i in range(2):
        wsend[i] = acc[i].astype(BF).reshape(NZ, FZ, W)
    wout = []
    for d in (4, 3, 5, 2, 6, 1, 7):
        t = zz(d)
        for i, ref in enumerate((gg_ref, ug_ref)):
            k = remote(
                wsend.at[i, t], ref.at[:, pl.ds(z * W, W)], gs.at[i, d], gr.at[i, d], {"et": t}
            )
            go(k)
            wout.append(k)
    for g in unsent:
        send_rows(g)
    for d in range(1, NZ):
        remote(sp.at[z], sp.at[z], sps.at[d], spr.at[d], {"et": zz(d)}).wait_recv()
    total = sp[0]
    for i in range(1, NZ):
        total = total + sp[i]
    stot[...] = total.reshape(NY, 1, 128)

    def send_scores(d, carry):
        score_to(lax.rem(e + d, NE)).start()
        return carry

    lax.fori_loop(1, NE, send_scores, 0)
    keep = [
        pltpu.make_async_copy(rsend.at[y, x, c], back.at[e], lsem.at[0]),
        pltpu.make_async_copy(stot.at[y], sback.at[e], lsem.at[1]),
        pltpu.make_async_copy(wsend.at[0, z], gg_ref.at[:, pl.ds(z * W, W)], lsem.at[2]),
        pltpu.make_async_copy(wsend.at[1, z], ug_ref.at[:, pl.ds(z * W, W)], lsem.at[3]),
    ]
    for k in keep:
        k.start()

    hs = jnp.concatenate([hsp[b] for b in range(NY)], axis=1)
    for f in range(NZ):
        rows = row_grad[:, :, f * W : (f + 1) * W].reshape(1024, W)
        down[:, f * W : (f + 1) * W] = dot(hs, rows).astype(BF)
    out_down = pltpu.make_async_copy(down, dg_ref, lsem.at[4])
    out_down.start()

    ids = ids_ref[...]
    row_e = lax.broadcasted_iota(jnp.int32, (NE, TOK), 0)
    names = jnp.zeros((NE, TOK), F32)
    for k in range(TOP):
        names += (ids[k : k + 1, :] == row_e).astype(F32)
    ti = lax.broadcasted_iota(jnp.int32, (TOK, TOK), 0)
    tj = lax.broadcasted_iota(jnp.int32, (TOK, TOK), 1)
    rank = dot(names.astype(BF), (ti < tj).astype(F32).astype(BF))
    rank = jnp.where(names > 0, rank, -1.0)
    ei = lax.broadcasted_iota(jnp.int32, (1024, NE), 0)
    ej = lax.broadcasted_iota(jnp.int32, (1024, NE), 1)
    spread = (ei // 16 == ej).astype(F32).astype(BF)
    slot = lax.rem(lax.broadcasted_iota(jnp.int32, (1024, TOK), 0), 16).astype(F32)
    gather = (dot(spread, rank.astype(BF)) == slot).astype(F32).astype(BF)

    for k in keep:
        k.wait()

    def wait_back(d, carry):
        t = lax.rem(e + d, NE)
        rows_from(t).wait_recv()
        score_from(t).wait_recv()
        return carry

    lax.fori_loop(1, NE, wait_back, 0)
    tg_ref[...] = dot(gather, back[...].reshape(1024, W), ((0,), (0,))).astype(BF)
    li = lax.broadcasted_iota(jnp.int32, (16, 128), 0)
    lj = lax.broadcasted_iota(jnp.int32, (16, 128), 1)
    mine = (lj == x * 32 + c * 16 + li).astype(F32)
    slots = dot(sback[...].reshape(NE, 128), mine, ((1,), (1,)), lax.Precision.HIGHEST)
    value = jnp.zeros((NE, TOK), F32)
    for j in range(16):
        value += jnp.where(rank == j, slots[:, j : j + 1], 0.0)
    for k in range(TOP):
        sg_ref[k : k + 1, :] = jnp.sum(
            jnp.where(ids[k : k + 1, :] == row_e, value, 0.0), axis=0, keepdims=True
        )

    out_down.wait()
    for k in wout:
        k.wait_recv()
    for k in pend:
        k.wait_send()

    def wait_sent(d, carry):
        t = lax.rem(e + d, NE)
        rows_to(t).wait_send()
        score_to(t).wait_send()
        return carry

    lax.fori_loop(1, NE, wait_sent, 0)


def publish(*refs):
    for i in range(5):
        refs[5 + i][...] = refs[i][...]


def body(
    out_grad, gate_scores, expert_ids, routed_rows, gate_pre, up_pre,
    gate_weight, up_weight, down_weight,
):
    vmem = pl.BlockSpec(memory_space=pltpu.VMEM)
    hbm = pl.BlockSpec(memory_space=pl.ANY)
    dma = pltpu.SemaphoreType.DMA
    outs = pl.pallas_call(
        kernel,
        out_shape=(
            jax.ShapeDtypeStruct((TOK, W), BF),
            jax.ShapeDtypeStruct((TOP, TOK), F32),
            jax.ShapeDtypeStruct((FZ, D), BF),
            jax.ShapeDtypeStruct((FZ, D), BF),
            jax.ShapeDtypeStruct((FZ, D), BF),
        ),
        in_specs=[hbm, vmem, vmem] + [hbm] * 6,
        out_specs=(vmem, vmem, hbm, hbm, hbm),
        scratch_shapes=[
            pltpu.VMEM((NY, NX, NC, NR, W), BF),
            pltpu.VMEM((2, NZ, FZ, W), BF),
            pltpu.VMEM((NY, NX, 32, W), BF),
            pltpu.VMEM((FZ, 1024), BF),
            pltpu.VMEM((FZ, 1024), BF),
            pltpu.VMEM((FZ, D), BF),
            pltpu.VMEM((NY, 2 * FZ, 128), BF),
            pltpu.VMEM((NY, 128, D), BF),
            pltpu.VMEM((NY, FZ, 128), BF),
            pltpu.VMEM((NY, NZ, 2 * FZ, 128), BF),
            pltpu.VMEM((NZ, NY, 128), F32),
            pltpu.VMEM((NY, 1, 128), F32),
            pltpu.VMEM((2, FF, W), F32),
            pltpu.VMEM((2, NZ, FZ, W), BF),
            pltpu.VMEM((FZ, D), BF),
            pltpu.VMEM((NY, NX, NC, 16, W), BF),
            pltpu.VMEM((NE, 16, W), BF),
            pltpu.VMEM((NE, 1, 128), F32),
            dma((14,)),
            dma((8,)), dma((8,)),
            dma((2, 8)), dma((2, 8)),
            dma((2, 2, 2)), dma((2, 2, 2)),
            dma((2, 5)), dma((2, 5)),
            dma((2, 8, 3)), dma((2, 8, 3)),
            dma((2, 3)), dma((2, 3)),
            dma((2, 4, 5)), dma((2, 4, 5)),
            dma((2, 8)), dma((2, 8)),
            dma((2, 8, 5)), dma((2, 8, 5)),
            dma((8,)), dma((8,)),
            dma((2, 8)), dma((2, 8)),
            dma((NE,)), dma((NE,)),
            dma((NE,)), dma((NE,)),
        ],
        compiler_params=pltpu.CompilerParams(
            collective_id=0, has_side_effects=True, vmem_limit_bytes=56 << 20
        ),
        name="expert_backward",
    )(
        out_grad, expert_ids.T, gate_scores.T, routed_rows.reshape(NX, NY, 32, W),
        gate_pre.reshape(FZ, 1024), up_pre.reshape(FZ, 1024),
        gate_weight.reshape(FZ, D), up_weight.reshape(FZ, D), down_weight.reshape(FZ, D),
    )
    outs = pl.pallas_call(
        publish,
        out_shape=tuple(jax.ShapeDtypeStruct(o.shape, o.dtype) for o in outs),
        in_specs=[vmem] * 5,
        out_specs=(vmem,) * 5,
        name="publish",
    )(*outs)
    token_grad, score_grad, gate_out, up_out, down_out = outs
    return token_grad, score_grad.T, gate_out[None], up_out[None], down_out[None]


def solution(mesh):
    return jax.shard_map(
        body,
        mesh=mesh,
        in_specs=(
            P("exp", "et"), P("exp", None), P("exp", None), P("exp", None, "et"),
            P("exp", "et", None), P("exp", "et", None), P("exp", "et", None),
            P("exp", "et", None), P("exp", "et", None),
        ),
        out_specs=(
            P("exp", "et"), P("exp", None), P("exp", "et", None), P("exp", "et", None),
            P("exp", "et", None),
        ),
        check_vma=False,
    )
```
